1024 devices in a mesh: tok: 16 (over x_lo, y), dmod: 4 (over x_hi, core), hid: 16 (over z).
Axes of the slice: x: 4 (x_hi: 2, x_lo: 2; x = x_hi * 2 + x_lo), y: 8, z: 16, core: 2. Of those that a mesh axis runs over, the one named last changes fastest.
Arguments:
- inputs: bfloat16 [1536, 8192], P('dmod', 'tok'), may hold values from -6 to 6
- grad_hidden: bfloat16 [1536, 14336], P('dmod', 'hid'), may hold values from -6 to 6
- gate_weight: bfloat16 [8192, 14336], P(('tok', 'dmod'), 'hid'), may hold values from -0.0625 to 0.0625
- up_weight: bfloat16 [8192, 14336], P(('tok', 'dmod'), 'hid'), may hold values from -0.0625 to 0.0625
Outputs:
- grad_inputs: bfloat16 [1536, 8192], P(('dmod', 'hid'), 'tok')
- grad_gate_weight: bfloat16 [8192, 14336], P(('tok', 'dmod'), 'hid')
- grad_up_weight: bfloat16 [8192, 14336], P(('tok', 'dmod'), 'hid')
The draws below stay inside these ranges and needn't reach their ends.
All inputs are finite; a program needn't handle non-finite values.
Results may differ from the reference program's by a relative error of at most 0.0049.
Values may be sent and summed in bfloat16 or wider, within the bound.
A program may use at most 32 MiB of HBM per device.

```python
import jax
import jax.numpy as jnp

D = 8192
FF = 14336
TOKENS = 1536


def level_of(rng, dims, shards, least, largest):
    def one(axis_at, shards_of):
        heights = jax.random.uniform(jax.random.fold_in(jax.random.fold_in(rng, 6), axis_at), (shards_of,), jnp.float32, least / len(shards), largest / len(shards))
        return jnp.repeat(jnp.exp(heights), dims[axis_at] // shards_of).reshape((-1,) + (1,) * (len(dims) - axis_at - 1))

    level = one(*shards[0])
    for cut in shards[1:]:
        level = level * one(*cut)
    return level


def noise(own_key, dims, scale, bound, pieces=(), dtype=jnp.bfloat16):
    result = scale * jax.random.normal(own_key, dims, jnp.float32)
    if pieces:
        result = result * level_of(own_key, dims, pieces, -0.22, 0.18)
    return jnp.clip(result, -bound, bound).astype(dtype)


def setup_inputs(seed: int = 0) -> dict:
    arg_keys = jax.random.split(jax.random.key(seed), 5)
    inputs = noise(arg_keys[0], (TOKENS, D), 1.0, 6.0, ((0, 4), (1, 16)))
    grad_hidden = noise(arg_keys[1], (TOKENS, FF), 1.0, 6.0, ((0, 4), (1, 16)))
    gate_weight = noise(arg_keys[2], (D, FF), D ** -0.5, 0.0625, ((0, 64), (1, 16)))
    up_weight = noise(arg_keys[3], (D, FF), D ** -0.5, 0.0625, ((0, 64), (1, 16)))
    return dict(inputs=inputs, grad_hidden=grad_hidden, gate_weight=gate_weight, up_weight=up_weight)


def reference(inputs, grad_hidden, gate_weight, up_weight):
    gate = jnp.dot(inputs, gate_weight, preferred_element_type=jnp.float32)
    up = jnp.dot(inputs, up_weight, preferred_element_type=jnp.float32)
    sigma = jax.nn.sigmoid(gate)
    upstream = grad_hidden.astype(jnp.float32)
    grad_gate = (upstream * up * sigma * (1.0 + gate * (1.0 - sigma))).astype(jnp.bfloat16)
    grad_up = (upstream * gate * sigma).astype(jnp.bfloat16)
    grad_inputs = jnp.dot(grad_gate, gate_weight.T, preferred_element_type=jnp.float32)
    grad_inputs = grad_inputs + jnp.dot(grad_up, up_weight.T, preferred_element_type=jnp.float32)
    grad_gate_weight = jnp.dot(inputs.T, grad_gate, preferred_element_type=jnp.float32)
    grad_up_weight = jnp.dot(inputs.T, grad_up, preferred_element_type=jnp.float32)
    return (grad_inputs.astype(jnp.bfloat16), grad_gate_weight.astype(jnp.bfloat16), grad_up_weight.astype(jnp.bfloat16))
```

```python
import functools

import jax
import jax.numpy as jnp
from jax import lax
from jax.experimental import pallas as pl
from jax.experimental.pallas import tpu as pltpu
from jax.sharding import PartitionSpec as P

BF, F32 = jnp.bfloat16, jnp.float32
LANES = 128


def contract(a, b, dims):
    return lax.dot_general(a, b, (dims, ((), ())), preferred_element_type=F32)


def widths(columns):
    tiles = columns // LANES
    return [2 * LANES] * (tiles // 2) + [LANES] * (tiles % 2)


def kernel(ny, nz, cols, x_ref, gh_ref, wg_ref, wu_ref, dx_ref, dwg_ref, dwu_ref, *scratch):
    n = len(cols)
    starts = [sum(cols[:i]) for i in range(n)]
    it = iter(scratch)
    take = lambda count: [next(it) for _ in range(count)]
    xs, xg, xt, ghs, zf, zs, zr, ze, fx = take(9)
    wb, pb, pr, yo, ys, yr, gb, dwf, dws, dwr = (take(n) for _ in range(10))
    x_s, x_r, gh_s, gh_r, z_s, z_r, f_s, f_r = take(8)
    w_s, w_r, p_s, p_r, y_s, y_r, g_s, g_r, k_s, k_r, d_s, d_r = take(12)

    tok, dmod, z = lax.axis_index("tok"), lax.axis_index("dmod"), lax.axis_index("hid")
    xl, y, xh, c = tok // ny, tok % ny, dmod // 2, dmod % 2
    other = 1 - c
    q = 2 * xl + xh
    tokens = x_ref.shape[0]
    share = tokens // (2 * ny)
    rows = tokens // nz
    home = c == xl

    def at(xl_=xl, xh_=xh, y_=y, c_=c, z_=z):
        return {"tok": xl_ * ny + y_, "dmod": xh_ * 2 + c_, "hid": z_}

    def send(src, dst, send_sem, recv_sem, target):
        copy = pltpu.make_async_remote_copy(
            src_ref=src, dst_ref=dst, send_sem=send_sem, recv_sem=recv_sem,
            device_id=target, device_id_type=pl.DeviceIdType.MESH,
        )
        copy.start()
        return copy

    def arrived(dst, sem):
        pltpu.make_async_copy(dst, dst, sem).wait()

    def block_of(k):
        qk = (q + k) % 4
        return qk, dict(xl_=qk // 2, xh_=qk % 2)

    pending = []

    barrier = pltpu.get_barrier_semaphore()
    peers = [at(c_=other), at(xl_=1 - xl, c_=other)]
    peers += [at(**block_of(k)[1]) for k in (1, 2, 3)]
    peers += [at(y_=(y + k) % ny) for k in range(1, ny)]
    peers += [at(z_=(z + k) % nz) for k in range(1, nz)]
    for peer in peers:
        pl.semaphore_signal(barrier, 1, device_id=peer, device_id_type=pl.DeviceIdType.MESH)

    for h in range(2):
        for cc in range(2):
            at_col = (2 * h + cc) * LANES
            xs[cc, h] = x_ref[:, at_col : at_col + LANES]
    for i in range(n):
        span = slice(starts[i], starts[i] + cols[i])
        wb[i][0, q] = wg_ref[:, span]
        wb[i][1, q] = wu_ref[:, span]

    @pl.when(home)
    def _():
        xg[xl] = xs[c]
        ghs[...] = gh_ref[c]

    pl.semaphore_wait(barrier, len(peers))

    to_core = (xs.at[other], xg.at[xl], x_s.at[0], x_r.at[0], at(c_=other))
    to_gh = (gh_ref.at[other], ghs, gh_s, gh_r, at(c_=other))
    to_chip = [
        (xs.at[cc], xg.at[xl], x_s.at[cc], x_r.at[1], at(xl_=1 - xl, c_=cc)) for cc in range(2)
    ]

    @pl.when(home)
    def _():
        send(*to_core)
        send(*to_gh)

    @pl.when(jnp.logical_not(home))
    def _():
        for args in to_chip:
            send(*args)

    for i in range(n):
        for k in (1, 3, 2):
            target = at(**block_of(k)[1])
            pending.append(
                send(wb[i].at[:, q], wb[i].at[:, q], w_s.at[i, k - 1], w_r.at[i, k - 1], target)
            )

    arrived(xg.at[1 - xl], x_r.at[1])

    @pl.when(jnp.logical_not(home))
    def _():
        arrived(xg.at[xl], x_r.at[0])
        arrived(ghs, gh_r)

    for b in range(4):
        xt[b] = xg[b // 2, b % 2].astype(F32).T.astype(BF)

    def partial(i):
        for k in (1, 2, 3):
            qk = (q + 4 - k) % 4
            arrived(wb[i].at[:, qk], w_r.at[i, k - 1])
        wide = jnp.concatenate([xg[b // 2, b % 2] for b in range(4)], axis=1)
        for m in range(2):
            w = wb[i][m].reshape(4 * LANES, cols[i])
            part = contract(wide, w, ((1,), (0,))).reshape(2, ny, share, cols[i])
            pb[i][:, :, m * share : (m + 1) * share] = part
        pending.append(send(pb[i].at[other], pr[i], p_s.at[i], p_r.at[i], at(c_=other)))

    def scatter(i):
        arrived(pr[i], p_r.at[i])
        ys[i][...] = (pb[i][c] + pr[i][...]).astype(BF)
        yo[i][...] = pb[i][c, y] + pr[i][y]
        for k in far_first:
            yk = (y + k) % ny
            pending.append(
                send(ys[i].at[yk], yr[i].at[k - 1], y_s.at[i, k - 1], y_r.at[i, k - 1], at(y_=yk))
            )

    far_first = sorted(range(1, ny), key=lambda k: -min(k, ny - k))

    def activate(i):
        total = yo[i][...]
        for k in far_first[::-1]:
            arrived(yr[i].at[k - 1], y_r.at[i, k - 1])
            total = total + yr[i][k - 1].astype(F32)
        gate, up = total[:share], total[share:]
        up_grad = ghs[:, starts[i] : starts[i] + cols[i]]
        sigma = jax.nn.sigmoid(gate)
        grad_gate = up_grad * up * sigma * (1.0 + gate * (1.0 - sigma))
        grad_up = up_grad * gate * sigma
        gb[i][c, y] = jnp.concatenate([grad_gate, grad_up], axis=0).astype(BF)
        for k in far_first:
            yk = (y + k) % ny
            block = gb[i].at[c, y]
            pending.append(send(block, block, g_s.at[i, k - 1], g_r.at[i, k - 1], at(y_=yk)))

    def gather(i):
        for k in far_first[::-1]:
            arrived(gb[i].at[c, (y + ny - k) % ny], g_r.at[i, k - 1])
        pending.append(send(gb[i].at[c], gb[i].at[c], k_s.at[i], k_r.at[i], at(c_=other)))

    def grads_of(i):
        both = gb[i][...].astype(F32).reshape(2 * ny, 2 * share, cols[i])
        grad_gate = both[:, :share].reshape(tokens, cols[i]).astype(BF)
        grad_up = both[:, share:].reshape(tokens, cols[i]).astype(BF)
        return grad_gate, grad_up

    def input_part(i):
        arrived(gb[i].at[other], k_r.at[i])
        for b in range(4):
            total = 0.0
            for m, grad in enumerate(grads_of(i)):
                total = total + contract(grad, wb[i][m, b], ((1,), (1,)))
            total = total.reshape(nz, rows, LANES)
            span = slice(b * rows, (b + 1) * rows)
            zf[:, span] = total if i == 0 else zf[:, span] + total

    def weight_part(i):
        for m, grad in enumerate(grads_of(i)):
            for b in range(4):
                dwf[i][b, m] = contract(xt[b], grad, ((1,), (0,)))
        dws[i][...] = dwf[i][...].astype(BF)
        for k in (2, 1, 3):
            qk, where = block_of(k)
            pending.append(
                send(dws[i].at[qk], dwr[i].at[k - 1], d_s.at[i, k - 1], d_r.at[i, k - 1], at(**where))
            )

    def weight_out(i):
        total = dwf[i][q]
        for k in (1, 3, 2):
            arrived(dwr[i].at[k - 1], d_r.at[i, k - 1])
            total = total + dwr[i][k - 1].astype(F32)
        span = slice(starts[i], starts[i] + cols[i])
        dwg_ref[:, span] = total[0].astype(BF)
        dwu_ref[:, span] = total[1].astype(BF)

    stages = [partial, scatter, activate, gather, input_part, weight_part]
    order = []
    for i in range(n):
        for at_step, stage in zip((0, 0.1, 1.2, 2.3, 2.4, 2.5), stages):
            order.append((i + at_step, i, stage))
    for _, i, stage in sorted(order, key=lambda entry: entry[0]):
        if i == n - 1 and stage is weight_part:
            z_far = sorted(range(1, nz), key=lambda k: -min(k, nz - k))
            zs[...] = zf[...].astype(BF)
            for k in z_far:
                zk = (z + k) % nz
                pending.append(
                    send(zs.at[zk], zr.at[k - 1], z_s.at[k - 1], z_r.at[k - 1], at(z_=zk))
                )
        stage(i)
    for i in range(n):
        weight_out(i)

    total = zf[z]
    for k in z_far[::-1]:
        arrived(zr.at[k - 1], z_r.at[k - 1])
        total = total + zr[k - 1].astype(F32)
    half = 2 * rows
    ze[...] = total.astype(BF).reshape(2, half, LANES)
    mine, theirs = ze.at[xl], ze.at[1 - xl]
    last = send(theirs, fx.at[c], f_s.at[0], f_r.at[c], at(xl_=1 - xl, c_=xl))
    on_chip = (mine, fx.at[c], f_s.at[1], f_r.at[c], at(c_=other))

    @pl.when(home)
    def _():
        fx[c] = ze[xl]

    @pl.when(jnp.logical_not(home))
    def _():
        send(*on_chip)
        arrived(fx.at[c], f_r.at[c])

    arrived(fx.at[other], f_r.at[other])
    for cc in range(2):
        got = fx[cc].astype(F32)
        for h in range(2):
            at_col = (2 * h + cc) * LANES
            dx_ref[:, at_col : at_col + LANES] = got[h * rows : (h + 1) * rows].astype(BF)

    def sent(src, sem):
        pltpu.make_async_copy(src, src, sem).wait()

    @pl.when(home)
    def _():
        sent(xs.at[other], x_s.at[0])
        sent(gh_ref.at[other], gh_s)

    @pl.when(jnp.logical_not(home))
    def _():
        for cc in range(2):
            sent(xs.at[cc], x_s.at[cc])
        sent(mine, f_s.at[1])

    last.wait_send()
    for copy in pending:
        copy.wait_send()


def shards(ny, nz, inputs, grad_hidden, gate_weight, up_weight):
    tokens, features = inputs.shape
    columns = gate_weight.shape[1]
    cols = widths(columns)
    n = len(cols)
    share, rows = tokens // (2 * ny), tokens // nz
    y = lax.axis_index("tok") % ny
    upstream = grad_hidden.reshape(2, ny, share, columns)
    upstream = lax.dynamic_index_in_dim(upstream, y, 1, keepdims=False).astype(F32)

    vmem = lambda shape, dtype: pltpu.VMEM(shape, dtype)
    scratch = [
        vmem((2, 2, tokens, LANES), BF),
        vmem((2, 2, tokens, LANES), BF),
        vmem((4, LANES, tokens), BF),
        vmem((share, columns), F32),
        vmem((nz, 4 * rows, LANES), F32),
        vmem((nz, 4 * rows, LANES), BF),
        vmem((nz - 1, 4 * rows, LANES), BF),
        vmem((2, 2 * rows, LANES), BF),
        vmem((2, 2 * rows, LANES), BF),
    ]
    for shape, dtype in (
        (lambda w: (2, 4, LANES, w), BF),
        (lambda w: (2, ny, 2 * share, w), F32),
        (lambda w: (ny, 2 * share, w), F32),
        (lambda w: (2 * share, w), F32),
        (lambda w: (ny, 2 * share, w), BF),
        (lambda w: (ny - 1, 2 * share, w), BF),
        (lambda w: (2, ny, 2 * share, w), BF),
        (lambda w: (4, 2, LANES, w), F32),
        (lambda w: (4, 2, LANES, w), BF),
        (lambda w: (3, 2, LANES, w), BF),
    ):
        scratch += [vmem(shape(w), dtype) for w in cols]
    dma = pltpu.SemaphoreType.DMA
    scratch += [dma((2,)), dma((2,)), dma, dma, dma((nz - 1,)), dma((nz - 1,)), dma((2,)), dma((2,))]
    for shape in ((n, 3), (n,), (n, ny - 1), (n, ny - 1), (n,), (n, 3)):
        scratch += [dma(shape), dma(shape)]

    in_vmem = pl.BlockSpec(memory_space=pltpu.VMEM)
    return pl.pallas_call(
        functools.partial(kernel, ny, nz, cols),
        out_shape=(
            jax.ShapeDtypeStruct((rows, features), BF),
            jax.ShapeDtypeStruct(gate_weight.shape, BF),
            jax.ShapeDtypeStruct(up_weight.shape, BF),
        ),
        in_specs=[in_vmem] * 4,
        out_specs=(in_vmem,) * 3,
        scratch_shapes=scratch,
        compiler_params=pltpu.CompilerParams(
            collective_id=0, has_side_effects=True, vmem_limit_bytes=40 * 2**20
        ),
        name="step",
    )(inputs, upstream, gate_weight, up_weight)


def solution(mesh):
    placed = (
        P("dmod", "tok"),
        P("dmod", "hid"),
        P(("tok", "dmod"), "hid"),
        P(("tok", "dmod"), "hid"),
    )
    return jax.shard_map(
        functools.partial(shards, mesh.shape["tok"] // 2, mesh.shape["hid"]),
        mesh=mesh,
        in_specs=placed,
        out_specs=(P(("dmod", "hid"), "tok"), P(("tok", "dmod"), "hid"), P(("tok", "dmod"), "hid")),
        check_vma=False,
    )
```

```python
import functools

import jax
import jax.numpy as jnp
from jax import lax
from jax.experimental import pallas as pl
from jax.experimental.pallas import tpu as pltpu
from jax.sharding import PartitionSpec as P

BF, F32 = jnp.bfloat16, jnp.float32
LANES = 128
GROUP = 4
SIGNS = (1, -1)


def contract(a, b, dims):
    return lax.dot_general(a, b, (dims, ((), ())), preferred_element_type=F32)


def widths(columns):
    tiles = columns // LANES
    return [2 * LANES] * (tiles // 2) + [LANES] * (tiles % 2)


def kernel(ny, nz, cols, x_ref, gh_ref, wg_ref, wu_ref, dx_ref, dwg_ref, dwu_ref, *scratch):
    n = len(cols)
    starts = [sum(cols[:i]) for i in range(n)]
    it = iter(scratch)
    take = lambda count: [next(it) for _ in range(count)]
    xs, xg, xt, ghw, zf, zs, ze, fx = take(8)
    z_far, z_near, z_anti, z_hub, z_hubs = take(5)
    wb, pb, pr, ys, gb, dwf, dws, dwr, dwh = (take(n) for _ in range(9))
    y_far, y_near, y_anti, y_hub, y_hubs = (take(n) for _ in range(5))
    in_s, x_s, x_r, t_s, t_r, gh_s, gh_r, f_s, f_r = take(9)
    w_s, w_r, p_s, p_r, ys_s, ys_r, g_s, g_r, k_s, k_r, d_s, d_r, zs_s, zs_r = take(14)

    tok, dmod, z = lax.axis_index("tok"), lax.axis_index("dmod"), lax.axis_index("hid")
    xl, y, xh, c = tok // ny, tok % ny, dmod // 2, dmod % 2
    other = 1 - c
    x = dmod - c + xl
    q = 2 * xl + xh
    tokens = x_ref.shape[0]
    share = tokens // (2 * ny)
    rows = tokens // nz
    home = c == xl

    def at(xl_=xl, xh_=xh, y_=y, c_=c, z_=z):
        return {"tok": xl_ * ny + y_, "dmod": xh_ * 2 + c_, "hid": z_}

    def along_x(k):
        xk = (x + 4 + k) % 4
        return 2 * (xk % 2) + xk // 2, at(xl_=xk % 2, xh_=xk // 2)

    def along(axis, k):
        if axis == "y":
            return (y + ny + k) % ny
        return (z + nz + k) % nz

    def there(axis, k):
        return at(y_=along("y", k)) if axis == "y" else at(z_=along("z", k))

    def send(src, dst, send_sem, recv_sem, target):
        copy = pltpu.make_async_remote_copy(
            src_ref=src, dst_ref=dst, send_sem=send_sem, recv_sem=recv_sem,
            device_id=target, device_id_type=pl.DeviceIdType.MESH,
        )
        copy.start()
        return copy

    def arrived(dst, sem):
        pltpu.make_async_copy(dst, dst, sem).wait()

    sent = arrived
    pending = []

    barrier = pltpu.get_barrier_semaphore()
    y_hops, z_hops = ny // 4, nz // 4
    y_off = sorted({s * k % ny for k in range(1, y_hops + 1) for s in SIGNS})
    z_off = sorted({s * k % nz for k in range(1, max(z_hops, GROUP - 1) + 1) for s in SIGNS} - {0})
    peers = [at(c_=other), at(xl_=1 - xl, c_=other)]
    peers += [along_x(k)[1] for k in (1, 2, 3)]
    peers += [there("y", k) for k in y_off] + [there("z", k) for k in z_off]
    for peer in peers:
        pl.semaphore_signal(barrier, 1, device_id=peer, device_id_type=pl.DeviceIdType.MESH)

    local = []

    def bring(src, dst):
        copy = pltpu.make_async_copy(src, dst, in_s.at[len(local)])
        copy.start()
        local.append(copy)

    for i in range(n):
        span = pl.ds(starts[i], cols[i])
        bring(wg_ref.at[:, span], wb[i].at[0, q])
        bring(wu_ref.at[:, span], wb[i].at[1, q])
    for h in range(2):
        for cc in range(2):
            bring(x_ref.at[:, pl.ds((2 * h + cc) * LANES, LANES)], xs.at[cc, h])

    def window(core):
        turn = core * ny + y
        first = pl.multiple_of(2 * share * (turn // 2) + 16 * (turn % 2), 16)
        return gh_ref.at[pl.ds(first, 32), :]

    own_gh = pltpu.make_async_copy(window(c), ghw, gh_r)

    @pl.when(home)
    def _():
        own_gh.start()

    for copy in local:
        copy.wait()

    @pl.when(home)
    def _():
        xg[xl] = xs[c]

    pl.semaphore_wait(barrier, len(peers))

    def weights_out(i):
        own = wb[i].at[:, q]
        for slot, k in enumerate(SIGNS):
            pending.append(send(own, own, w_s.at[i, slot], w_r.at[i, slot], along_x(k)[1]))

    part = tokens // GROUP
    turn = z % GROUP

    def part_of(slab, j):
        return slab.at[:, pl.ds(pl.multiple_of(j * part, part), part)]

    to_core = (xs.at[other], xg.at[xl], x_s.at[0], x_r.at[0], at(c_=other))
    to_gh = (window(other), ghw, gh_s, gh_r, at(c_=other))
    to_chip = [
        (part_of(xs.at[cc], turn), part_of(xg.at[xl], turn), x_s.at[cc], x_r.at[1],
         at(xl_=1 - xl, c_=cc))
        for cc in range(2)
    ]

    @pl.when(home)
    def _():
        send(*to_core)
        send(*to_gh)

    @pl.when(jnp.logical_not(home))
    def _():
        for args in to_chip:
            send(*args)

    weights_out(0)
    weights_out(1)

    def features():
        mine = part_of(xg.at[1 - xl], turn)
        arrived(mine, x_r.at[1])
        for k in range(1, GROUP):
            mate = z - turn + (turn + k) % GROUP
            pending.append(send(mine, mine, t_s.at[k - 1], t_r.at[k - 1], at(z_=mate)))

    def features_done():
        for k in range(1, GROUP):
            arrived(part_of(xg.at[1 - xl], (turn + GROUP - k) % GROUP), t_r.at[k - 1])

        @pl.when(jnp.logical_not(home))
        def _():
            arrived(xg.at[xl], x_r.at[0])

        for b in range(4):
            xt[b] = xg[b // 2, b % 2].astype(F32).T.astype(BF)

    def weights_on(i):
        for slot, k in enumerate(SIGNS):
            qk = along_x(-k)[0]
            arrived(wb[i].at[:, qk], w_r.at[i, slot])
            block = wb[i].at[slot, qk]
            pending.append(
                send(block, block, w_s.at[i, 2 + slot], w_r.at[i, 2 + slot], along_x(k)[1])
            )
        if i + 2 < n:
            weights_out(i + 2)

    def partial(i):
        qk = along_x(2)[0]
        for slot in range(2):
            arrived(wb[i].at[slot, qk], w_r.at[i, 2 + slot])
        wide = jnp.concatenate([xg[b // 2, b % 2] for b in range(4)], axis=1)
        for m in range(2):
            w = wb[i][m].reshape(4 * LANES, cols[i])
            block = contract(wide, w, ((1,), (0,))).reshape(2, ny, share, cols[i])
            pb[i][:, :, m * share : (m + 1) * share] = block
        pending.append(send(pb[i].at[other], pr[i], p_s.at[i], p_r.at[i], at(c_=other)))

    def reduce_start(axis, hops, src, far, near, anti, s_sem, r_sem):
        pick = lambda k: src.at[along(axis, k)]
        way = 2 * (along(axis, 0) % 2) - 1
        for j in range(hops - 1, 0, -1):
            for si, s in enumerate(SIGNS):
                slot = si * (hops - 1) + j - 1
                pending.append(
                    send(pick(s * (j + hops)), far.at[si, j - 1], s_sem.at[slot], r_sem.at[slot],
                         there(axis, s * j))
                )
        slot = 2 * (hops - 1)
        pending.append(
            send(pick(2 * hops), anti, s_sem.at[slot], r_sem.at[slot], there(axis, way * hops))
        )
        for j in range(1, hops):
            for si, s in enumerate(SIGNS):
                slot = (2 + si) * (hops - 1) + j
                pending.append(
                    send(pick(s * j), near.at[si, j - 1], s_sem.at[slot], r_sem.at[slot],
                         there(axis, s * j))
                )

    def reduce_relay(axis, hops, own, far, anti, hub, hubs, s_sem, r_sem):
        odd = along(axis, 0) % 2
        for j in range(1, hops):
            for si in range(2):
                arrived(far.at[si, j - 1], r_sem.at[si * (hops - 1) + j - 1])
        arrived(anti, r_sem.at[2 * (hops - 1)])
        for first in (True, False):
            si = 1 - odd if first else odd
            way = 1 - 2 * si
            total = own(along(axis, way * hops))
            for j in range(1, hops):
                total = total + far[si, j - 1].astype(F32)
            if first:
                total = total + anti[...].astype(F32)
            hubs[si] = total.astype(BF)
            slot = 4 * (hops - 1) + 1
            pending.append(
                send(hubs.at[si], hub.at[si], s_sem.at[slot + si], r_sem.at[slot + si],
                     there(axis, way * hops))
            )

    def reduce_end(axis, hops, own, near, hub, r_sem):
        total = own(along(axis, 0))
        for j in range(1, hops):
            for si in range(2):
                arrived(near.at[si, j - 1], r_sem.at[(2 + si) * (hops - 1) + j])
                total = total + near[si, j - 1].astype(F32)
        for si in range(2):
            arrived(hub.at[si], r_sem.at[4 * (hops - 1) + 1 + si])
            total = total + hub[si].astype(F32)
        return total

    def own_sum(i):
        return lambda yk: pb[i][c, yk] + pr[i][yk]

    def scatter(i):
        arrived(pr[i], p_r.at[i])
        ys[i][...] = (pb[i][c] + pr[i][...]).astype(BF)
        reduce_start("y", y_hops, ys[i], y_far[i], y_near[i], y_anti[i], ys_s.at[i], ys_r.at[i])

    def relay(i):
        reduce_relay("y", y_hops, own_sum(i), y_far[i], y_anti[i], y_hub[i], y_hubs[i],
                     ys_s.at[i], ys_r.at[i])

    def activate(i):
        if i == 0:
            @pl.when(home)
            def _():
                own_gh.wait()

            @pl.when(jnp.logical_not(home))
            def _():
                arrived(ghw, gh_r)

        total = reduce_end("y", y_hops, own_sum(i), y_near[i], y_hub[i], ys_r.at[i])
        gate, up = total[:share], total[share:]
        upstream = ghw[:, starts[i] : starts[i] + cols[i]].astype(F32)
        upstream = jnp.where((c * ny + y) % 2 == 1, upstream[8 : 8 + share], upstream[:share])
        sigma = jax.nn.sigmoid(gate)
        grad_gate = upstream * up * sigma * (1.0 + gate * (1.0 - sigma))
        grad_up = upstream * gate * sigma
        gb[i][c, y] = jnp.concatenate([grad_gate, grad_up], axis=0).astype(BF)
        own = gb[i].at[c, y]
        for k in range(y_hops, 0, -1):
            for s in SIGNS:
                slot = s * k % ny - 1
                pending.append(send(own, own, g_s.at[i, slot], g_r.at[i, slot], there("y", s * k)))

    def spread(i):
        for s in SIGNS:
            block = gb[i].at[c, along("y", -s * y_hops)]
            arrived(block, g_r.at[i, s * y_hops % ny - 1])
            for j in range(1, y_hops):
                slot = s * (j + y_hops) % ny - 1
                pending.append(send(block, block, g_s.at[i, slot], g_r.at[i, slot], there("y", s * j)))
        way = 2 * (y % 2) - 1
        block = gb[i].at[c, along("y", -way * y_hops)]
        slot = 2 * y_hops - 1
        pending.append(
            send(block, block, g_s.at[i, slot], g_r.at[i, slot], there("y", way * y_hops))
        )

    def gather(i):
        for k in range(1, ny):
            if k not in (y_hops, ny - y_hops):
                arrived(gb[i].at[c, along("y", -k)], g_r.at[i, k - 1])
        pending.append(send(gb[i].at[c], gb[i].at[c], k_s.at[i], k_r.at[i], at(c_=other)))

    def grads_of(i):
        both = gb[i][...].astype(F32).reshape(2 * ny, 2 * share, cols[i])
        grad_gate = both[:, :share].reshape(tokens, cols[i]).astype(BF)
        grad_up = both[:, share:].reshape(tokens, cols[i]).astype(BF)
        return grad_gate, grad_up

    def input_part(i):
        arrived(gb[i].at[other], k_r.at[i])
        grads = grads_of(i)
        for b in range(4):
            total = 0.0
            for m, grad in enumerate(grads):
                total = total + contract(grad, wb[i][m, b], ((1,), (1,)))
            total = total.reshape(nz, rows, LANES)
            span = slice(b * rows, (b + 1) * rows)
            zf[:, span] = total if i == 0 else zf[:, span] + total

    def weight_part(i):
        for m, grad in enumerate(grads_of(i)):
            for b in range(4):
                dwf[i][b, m] = contract(xt[b], grad, ((1,), (0,)))
        dws[i][...] = dwf[i][...].astype(BF)
        q2 = along_x(2)[0]
        for m, k in enumerate(SIGNS):
            pending.append(
                send(dws[i].at[q2, m], dwr[i].at[m], d_s.at[i, m], d_r.at[i, m], along_x(k)[1])
            )
        for m, k in enumerate(SIGNS):
            qk, target = along_x(k)
            pending.append(
                send(dws[i].at[qk, 1 - m], dwr[i].at[2 + m], d_s.at[i, 2 + m], d_r.at[i, 2 + m], target)
            )

    def weight_relay(i):
        for m, k in enumerate(SIGNS):
            qk, target = along_x(k)
            arrived(dwr[i].at[m], d_r.at[i, m])
            dwh[i][m] = (dwf[i][qk, m] + dwr[i][m].astype(F32)).astype(BF)
            pending.append(
                send(dwh[i].at[m], dwr[i].at[4 + m], d_s.at[i, 4 + m], d_r.at[i, 4 + m], target)
            )

    def weight_out(i):
        span = slice(starts[i], starts[i] + cols[i])
        for m, out in enumerate((dwg_ref, dwu_ref)):
            total = dwf[i][q, m]
            for slot in (3 - m, 4 + m):
                arrived(dwr[i].at[slot], d_r.at[i, slot])
                total = total + dwr[i][slot].astype(F32)
            out[:, span] = total.astype(BF)

    own_input = lambda zk: zf[zk]

    def input_start():
        zs[...] = zf[...].astype(BF)
        reduce_start("z", z_hops, zs, z_far, z_near, z_anti, zs_s, zs_r)

    def input_relay():
        reduce_relay("z", z_hops, own_input, z_far, z_anti, z_hub, z_hubs, zs_s, zs_r)

    ready = {
        weights_on: (6, 9, 13, 16),
        partial: (10, 14, 17, 18),
        scatter: (12, 16.2, 19, 20),
        relay: (16, 20, 23, 24),
        activate: (20, 24, 27, 28),
        spread: (24.5, 29, 31.5, 32.5),
        gather: (28, 32.4, 35, 36),
        input_part: (29, 33, 36.5, 37),
        weight_part: (29.5, 33.5, 38, 38.1),
        weight_relay: (34.4, 38.2, 43, 44),
        weight_out: (40, 42, 48, 49),
    }
    late = {features: 5, features_done: 9.9, input_start: 37.1, input_relay: 45}
    order = [(when, stage, None) for stage, when in late.items()]
    for stage, times in ready.items():
        shift = len(times) - n
        order += [(times[i if i < n - 1 else i + shift], stage, i) for i in range(n)]
    for _, stage, i in sorted(order, key=lambda entry: entry[0]):
        stage() if i is None else stage(i)

    half = 2 * rows
    total = reduce_end("z", z_hops, own_input, z_near, z_hub, zs_r)
    ze[...] = total.astype(BF).reshape(2, half, LANES)
    last = send(ze.at[1 - xl], fx.at[c], f_s.at[0], f_r.at[c], at(xl_=1 - xl, c_=xl))

    @pl.when(home)
    def _():
        fx[c] = ze[xl]

    @pl.when(jnp.logical_not(home))
    def _():
        send(ze.at[xl], fx.at[c], f_s.at[1], f_r.at[c], at(c_=other))
        arrived(fx.at[c], f_r.at[c])

    arrived(fx.at[other], f_r.at[other])
    for cc in range(2):
        got = fx[cc].astype(F32)
        for h in range(2):
            at_col = (2 * h + cc) * LANES
            dx_ref[:, at_col : at_col + LANES] = got[h * rows : (h + 1) * rows].astype(BF)

    @pl.when(home)
    def _():
        sent(xs.at[other], x_s.at[0])
        sent(window(other), gh_s)

    @pl.when(jnp.logical_not(home))
    def _():
        for cc in range(2):
            sent(part_of(xs.at[cc], turn), x_s.at[cc])
        sent(ze.at[xl], f_s.at[1])

    last.wait_send()
    for copy in pending:
        copy.wait_send()


def shards(ny, nz, inputs, grad_hidden, gate_weight, up_weight):
    tokens, features = inputs.shape
    columns = gate_weight.shape[1]
    cols = widths(columns)
    n = len(cols)
    share, rows = tokens // (2 * ny), tokens // nz
    yh, zh = ny // 4, nz // 4

    vmem = lambda shape, dtype=BF: pltpu.VMEM(shape, dtype)

    def ring(hops, block):
        return [
            (2, max(hops - 1, 1)) + block,
            (2, max(hops - 1, 1)) + block,
            block,
            (2,) + block,
            (2,) + block,
        ]

    z_block = (4 * rows, LANES)
    scratch = [
        vmem((2, 2, tokens, LANES)),
        vmem((2, 2, tokens, LANES)),
        vmem((4, LANES, tokens)),
        vmem((32, columns)),
        vmem((nz,) + z_block, F32),
        vmem((nz,) + z_block),
        vmem((2, 2 * rows, LANES)),
        vmem((2, 2 * rows, LANES)),
    ]
    scratch += [vmem(shape) for shape in ring(zh, z_block)]
    for shape, dtype in (
        (lambda w: (2, 4, LANES, w), BF),
        (lambda w: (2, ny, 2 * share, w), F32),
        (lambda w: (ny, 2 * share, w), F32),
        (lambda w: (ny, 2 * share, w), BF),
        (lambda w: (2, ny, 2 * share, w), BF),
        (lambda w: (4, 2, LANES, w), F32),
        (lambda w: (4, 2, LANES, w), BF),
        (lambda w: (6, LANES, w), BF),
        (lambda w: (2, LANES, w), BF),
    ):
        scratch += [vmem(shape(w), dtype) for w in cols]
    for j in range(5):
        scratch += [vmem(ring(yh, (2 * share, w))[j]) for w in cols]
    dma = pltpu.SemaphoreType.DMA
    scratch += [dma((2 * n + 4,)), dma((2,)), dma((2,)), dma((GROUP - 1,)), dma((GROUP - 1,))]
    scratch += [dma, dma, dma((2,)), dma((2,))]
    for shape in ((n, 4), (n,), (n, 4 * yh - 1), (n, ny - 1), (n,), (n, 6), (4 * zh - 1,)):
        scratch += [dma(shape), dma(shape)]

    in_hbm = pl.BlockSpec(memory_space=pl.ANY)
    in_vmem = pl.BlockSpec(memory_space=pltpu.VMEM)
    return pl.pallas_call(
        functools.partial(kernel, ny, nz, cols),
        out_shape=(
            jax.ShapeDtypeStruct((rows, features), BF),
            jax.ShapeDtypeStruct(gate_weight.shape, BF),
            jax.ShapeDtypeStruct(up_weight.shape, BF),
        ),
        in_specs=[in_hbm] * 4,
        out_specs=(in_vmem,) * 3,
        scratch_shapes=scratch,
        compiler_params=pltpu.CompilerParams(
            collective_id=0, has_side_effects=True, vmem_limit_bytes=36 * 2**20
        ),
        name="step",
    )(inputs, grad_hidden, gate_weight, up_weight)


def solution(mesh):
    placed = (
        P("dmod", "tok"),
        P("dmod", "hid"),
        P(("tok", "dmod"), "hid"),
        P(("tok", "dmod"), "hid"),
    )
    return jax.shard_map(
        functools.partial(shards, mesh.shape["tok"] // 2, mesh.shape["hid"]),
        mesh=mesh,
        in_specs=placed,
        out_specs=(P(("dmod", "hid"), "tok"), P(("tok", "dmod"), "hid"), P(("tok", "dmod"), "hid")),
        check_vma=False,
    )
```

```python
import functools

import jax
import jax.numpy as jnp
from jax import lax
from jax.experimental import pallas as pl
from jax.experimental.pallas import tpu as pltpu
from jax.sharding import PartitionSpec as P

BF, F32 = jnp.bfloat16, jnp.float32
LANES = 128
GROUP = 4
SIGNS = (1, -1)


def contract(a, b, dims):
    return lax.dot_general(a, b, (dims, ((), ())), preferred_element_type=F32)


def widths(columns):
    tiles = columns // LANES
    return [2 * LANES] * (tiles // 2) + [LANES] * (tiles % 2)


def kernel(ny, nz, cols, x_ref, gh_ref, wg_ref, wu_ref, dx_ref, dwg_ref, dwu_ref, *scratch):
    n = len(cols)
    starts = [sum(cols[:i]) for i in range(n)]
    it = iter(scratch)
    take = lambda count: [next(it) for _ in range(count)]
    xs, xg, xt, ghw, zf, zs, ze, fx = take(8)
    z_far, z_near, z_anti, z_hub, z_hubs = take(5)
    wb, pb, pr, ys, gb, dwf, dws, dwr, dwh = (take(n) for _ in range(9))
    y_far, y_near, y_anti, y_hub, y_hubs = (take(n) for _ in range(5))
    in_s, x_s, x_r, t_s, t_r, gh_s, gh_r, f_s, f_r = take(9)
    w_s, w_r, p_s, p_r, ys_s, ys_r, g_s, g_r, k_s, k_r, d_s, d_r, zs_s, zs_r, e_s, e_r = take(16)

    tok, dmod, z = lax.axis_index("tok"), lax.axis_index("dmod"), lax.axis_index("hid")
    xl, y, xh, c = tok // ny, tok % ny, dmod // 2, dmod % 2
    other = 1 - c
    x = dmod - c + xl
    q = 2 * xl + xh
    tokens = x_ref.shape[0]
    share = tokens // (2 * ny)
    rows = tokens // nz
    home = c == xl

    def at(xl_=xl, xh_=xh, y_=y, c_=c, z_=z):
        return {"tok": xl_ * ny + y_, "dmod": xh_ * 2 + c_, "hid": z_}

    def along_x(k):
        xk = (x + 4 + k) % 4
        return 2 * (xk % 2) + xk // 2, at(xl_=xk % 2, xh_=xk // 2)

    def along(axis, k):
        if axis == "y":
            return (y + ny + k) % ny
        return (z + nz + k) % nz

    def there(axis, k):
        return at(y_=along("y", k)) if axis == "y" else at(z_=along("z", k))

    def send(src, dst, send_sem, recv_sem, target):
        copy = pltpu.make_async_remote_copy(
            src_ref=src, dst_ref=dst, send_sem=send_sem, recv_sem=recv_sem,
            device_id=target, device_id_type=pl.DeviceIdType.MESH,
        )
        copy.start()
        return copy

    def arrived(dst, sem):
        pltpu.make_async_copy(dst, dst, sem).wait()

    sent = arrived
    pending = []

    barrier = pltpu.get_barrier_semaphore()
    y_hops, z_hops = ny // 4, nz // 4
    y_off = sorted({s * k % ny for k in range(1, y_hops + 1) for s in SIGNS})
    z_off = sorted({s * k % nz for k in range(1, max(z_hops, GROUP - 1) + 1) for s in SIGNS} - {0})
    peers = [at(c_=other), at(xl_=1 - xl, c_=other)]
    peers += [along_x(k)[1] for k in (1, 2, 3)]
    peers += [there("y", k) for k in y_off] + [there("z", k) for k in z_off]
    for k in sorted({s * z_hops % nz for s in SIGNS}):
        for a, b in ((xl, other), (1 - xl, c), (1 - xl, other)):
            peers.append(at(xl_=a, c_=b, z_=along("z", k)))
    for peer in peers:
        pl.semaphore_signal(barrier, 1, device_id=peer, device_id_type=pl.DeviceIdType.MESH)

    local = []

    def bring(src, dst):
        copy = pltpu.make_async_copy(src, dst, in_s.at[len(local)])
        copy.start()
        local.append(copy)

    for i in range(n):
        span = pl.ds(starts[i], cols[i])
        bring(wg_ref.at[:, span], wb[i].at[0, q])
        bring(wu_ref.at[:, span], wb[i].at[1, q])
    for h in range(2):
        for cc in range(2):
            bring(x_ref.at[:, pl.ds((2 * h + cc) * LANES, LANES)], xs.at[cc, h])

    def window(core):
        turn = core * ny + y
        first = pl.multiple_of(2 * share * (turn // 2) + 16 * (turn % 2), 16)
        return gh_ref.at[pl.ds(first, 32), :]

    own_gh = pltpu.make_async_copy(window(c), ghw, gh_r)

    @pl.when(home)
    def _():
        own_gh.start()

    for copy in local:
        copy.wait()

    @pl.when(home)
    def _():
        xg[xl] = xs[c]

    pl.semaphore_wait(barrier, len(peers))

    def weights_out(i):
        own = wb[i].at[:, q]
        for slot, k in enumerate(SIGNS):
            pending.append(send(own, own, w_s.at[i, slot], w_r.at[i, slot], along_x(k)[1]))

    part = tokens // GROUP
    turn = z % GROUP

    def part_of(slab, j):
        return slab.at[:, pl.ds(pl.multiple_of(j * part, part), part)]

    to_core = (xs.at[other], xg.at[xl], x_s.at[0], x_r.at[0], at(c_=other))
    to_gh = (window(other), ghw, gh_s, gh_r, at(c_=other))
    to_chip = [
        (part_of(xs.at[cc], turn), part_of(xg.at[xl], turn), x_s.at[cc], x_r.at[1],
         at(xl_=1 - xl, c_=cc))
        for cc in range(2)
    ]

    @pl.when(home)
    def _():
        send(*to_core)
        send(*to_gh)

    @pl.when(jnp.logical_not(home))
    def _():
        for args in to_chip:
            send(*args)

    weights_out(0)
    weights_out(1)

    def features():
        mine = part_of(xg.at[1 - xl], turn)
        arrived(mine, x_r.at[1])
        for k in range(1, GROUP):
            mate = z - turn + (turn + k) % GROUP
            pending.append(send(mine, mine, t_s.at[k - 1], t_r.at[k - 1], at(z_=mate)))

    def features_done():
        for k in range(1, GROUP):
            arrived(part_of(xg.at[1 - xl], (turn + GROUP - k) % GROUP), t_r.at[k - 1])

        @pl.when(jnp.logical_not(home))
        def _():
            arrived(xg.at[xl], x_r.at[0])

        for b in range(4):
            xt[b] = xg[b // 2, b % 2].astype(F32).T.astype(BF)

    def weights_on(i):
        for slot, k in enumerate(SIGNS):
            qk = along_x(-k)[0]
            arrived(wb[i].at[:, qk], w_r.at[i, slot])
            block = wb[i].at[slot, qk]
            pending.append(
                send(block, block, w_s.at[i, 2 + slot], w_r.at[i, 2 + slot], along_x(k)[1])
            )
        if i + 2 < n:
            weights_out(i + 2)

    def partial(i):
        qk = along_x(2)[0]
        for slot in range(2):
            arrived(wb[i].at[slot, qk], w_r.at[i, 2 + slot])
        wide = jnp.concatenate([xg[b // 2, b % 2] for b in range(4)], axis=1)
        for m in range(2):
            w = wb[i][m].reshape(4 * LANES, cols[i])
            block = contract(wide, w, ((1,), (0,))).reshape(2, ny, share, cols[i])
            pb[i][:, :, m * share : (m + 1) * share] = block
        pending.append(send(pb[i].at[other], pr[i], p_s.at[i], p_r.at[i], at(c_=other)))

    def reduce_start(axis, hops, src, far, near, anti, s_sem, r_sem):
        pick = lambda k: src.at[along(axis, k)]
        way = 2 * (along(axis, 0) % 2) - 1
        for j in range(hops - 1, 0, -1):
            for si, s in enumerate(SIGNS):
                slot = si * (hops - 1) + j - 1
                pending.append(
                    send(pick(s * (j + hops)), far.at[si, j - 1], s_sem.at[slot], r_sem.at[slot],
                         there(axis, s * j))
                )
        slot = 2 * (hops - 1)
        pending.append(
            send(pick(2 * hops), anti, s_sem.at[slot], r_sem.at[slot], there(axis, way * hops))
        )
        for j in range(1, hops):
            for si, s in enumerate(SIGNS):
                slot = (2 + si) * (hops - 1) + j
                pending.append(
                    send(pick(s * j), near.at[si, j - 1], s_sem.at[slot], r_sem.at[slot],
                         there(axis, s * j))
                )

    def reduce_relay(axis, hops, own, far, anti, hubs, r_sem, deliver):
        odd = along(axis, 0) % 2
        for j in range(1, hops):
            for si in range(2):
                arrived(far.at[si, j - 1], r_sem.at[si * (hops - 1) + j - 1])
        arrived(anti, r_sem.at[2 * (hops - 1)])
        for first in (True, False):
            si = 1 - odd if first else odd
            way = 1 - 2 * si
            total = own(along(axis, way * hops))
            for j in range(1, hops):
                total = total + far[si, j - 1].astype(F32)
            if first:
                total = total + anti[...].astype(F32)
            hubs[si] = total.astype(BF)
            deliver(si, along(axis, way * hops))

    def reduce_near(axis, hops, own, near, r_sem):
        total = own(along(axis, 0))
        for j in range(1, hops):
            for si in range(2):
                arrived(near.at[si, j - 1], r_sem.at[(2 + si) * (hops - 1) + j])
                total = total + near[si, j - 1].astype(F32)
        return total

    def own_sum(i):
        return lambda yk: pb[i][c, yk] + pr[i][yk]

    def scatter(i):
        arrived(pr[i], p_r.at[i])
        ys[i][...] = (pb[i][c] + pr[i][...]).astype(BF)
        reduce_start("y", y_hops, ys[i], y_far[i], y_near[i], y_anti[i], ys_s.at[i], ys_r.at[i])

    y_slot = 4 * (y_hops - 1) + 1

    def relay(i):
        def deliver(si, yk):
            src, slot = y_hubs[i].at[si], y_slot + si
            pending.append(
                send(src, y_hub[i].at[si], ys_s.at[i, slot], ys_r.at[i, slot], at(y_=yk))
            )

        reduce_relay("y", y_hops, own_sum(i), y_far[i], y_anti[i], y_hubs[i], ys_r.at[i], deliver)

    def activate(i):
        if i == 0:
            @pl.when(home)
            def _():
                own_gh.wait()

            @pl.when(jnp.logical_not(home))
            def _():
                arrived(ghw, gh_r)

        total = reduce_near("y", y_hops, own_sum(i), y_near[i], ys_r.at[i])
        for si in range(2):
            arrived(y_hub[i].at[si], ys_r.at[i, y_slot + si])
            total = total + y_hub[i][si].astype(F32)
        gate, up = total[:share], total[share:]
        upstream = ghw[:, starts[i] : starts[i] + cols[i]].astype(F32)
        upstream = jnp.where((c * ny + y) % 2 == 1, upstream[8 : 8 + share], upstream[:share])
        sigma = jax.nn.sigmoid(gate)
        grad_gate = upstream * up * sigma * (1.0 + gate * (1.0 - sigma))
        grad_up = upstream * gate * sigma
        gb[i][c, y] = jnp.concatenate([grad_gate, grad_up], axis=0).astype(BF)
        own = gb[i].at[c, y]
        for k in range(y_hops, 0, -1):
            for s in SIGNS:
                slot = s * k % ny - 1
                pending.append(send(own, own, g_s.at[i, slot], g_r.at[i, slot], there("y", s * k)))

    def spread(i):
        for s in SIGNS:
            block = gb[i].at[c, along("y", -s * y_hops)]
            arrived(block, g_r.at[i, s * y_hops % ny - 1])
            for j in range(1, y_hops):
                slot = s * (j + y_hops) % ny - 1
                pending.append(send(block, block, g_s.at[i, slot], g_r.at[i, slot], there("y", s * j)))
        way = 2 * (y % 2) - 1
        block = gb[i].at[c, along("y", -way * y_hops)]
        slot = 2 * y_hops - 1
        pending.append(
            send(block, block, g_s.at[i, slot], g_r.at[i, slot], there("y", way * y_hops))
        )

    def gather(i):
        for k in range(1, ny):
            if k not in (y_hops, ny - y_hops):
                arrived(gb[i].at[c, along("y", -k)], g_r.at[i, k - 1])
        pending.append(send(gb[i].at[c], gb[i].at[c], k_s.at[i], k_r.at[i], at(c_=other)))

    def grads_of(i):
        both = gb[i][...].astype(F32).reshape(2 * ny, 2 * share, cols[i])
        grad_gate = both[:, :share].reshape(tokens, cols[i]).astype(BF)
        grad_up = both[:, share:].reshape(tokens, cols[i]).astype(BF)
        return grad_gate, grad_up

    def input_part(i):
        arrived(gb[i].at[other], k_r.at[i])
        grads = grads_of(i)
        for b in range(4):
            total = 0.0
            for m, grad in enumerate(grads):
                total = total + contract(grad, wb[i][m, b], ((1,), (1,)))
            total = total.reshape(nz, rows, LANES)
            span = slice(b * rows, (b + 1) * rows)
            zf[:, span] = total if i == 0 else zf[:, span] + total

    def weight_part(i):
        for m, grad in enumerate(grads_of(i)):
            for b in range(4):
                dwf[i][b, m] = contract(xt[b], grad, ((1,), (0,)))
        dws[i][...] = dwf[i][...].astype(BF)
        q2 = along_x(2)[0]
        for m, k in enumerate(SIGNS):
            pending.append(
                send(dws[i].at[q2, m], dwr[i].at[m], d_s.at[i, m], d_r.at[i, m], along_x(k)[1])
            )
        for m, k in enumerate(SIGNS):
            qk, target = along_x(k)
            pending.append(
                send(dws[i].at[qk, 1 - m], dwr[i].at[2 + m], d_s.at[i, 2 + m], d_r.at[i, 2 + m], target)
            )

    def weight_relay(i):
        for m, k in enumerate(SIGNS):
            qk, target = along_x(k)
            arrived(dwr[i].at[m], d_r.at[i, m])
            dwh[i][m] = (dwf[i][qk, m] + dwr[i][m].astype(F32)).astype(BF)
            pending.append(
                send(dwh[i].at[m], dwr[i].at[4 + m], d_s.at[i, 4 + m], d_r.at[i, 4 + m], target)
            )

    def weight_out(i):
        span = slice(starts[i], starts[i] + cols[i])
        for m, out in enumerate((dwg_ref, dwu_ref)):
            total = dwf[i][q, m]
            for slot in (3 - m, 4 + m):
                arrived(dwr[i].at[slot], d_r.at[i, slot])
                total = total + dwr[i][slot].astype(F32)
            out[:, span] = total.astype(BF)

    own_input = lambda zk: zf[zk]

    def input_start():
        zs[...] = zf[...].astype(BF)
        reduce_start("z", z_hops, zs, z_far, z_near, z_anti, zs_s, zs_r)

    half = 2 * rows

    def input_relay():
        def deliver(si, zk):
            for to in range(2):
                target = at(xl_=to, c_=xl, z_=zk)
                src = z_hubs.at[si, pl.ds(to * half, half)]
                pending.append(send(src, z_hub.at[si, c], e_s.at[si, to], e_r.at[si, c], target))

        reduce_relay("z", z_hops, own_input, z_far, z_anti, z_hubs, zs_r, deliver)

    def input_near():
        total = reduce_near("z", z_hops, own_input, z_near, zs_r)
        ze[...] = total.reshape(2, half, LANES)
        target = at(xl_=1 - xl, c_=xl)
        pending.append(send(ze.at[1 - xl], fx.at[c], f_s.at[0], f_r.at[c], target))

        @pl.when(home)
        def _():
            fx[c] = ze[xl]

        @pl.when(jnp.logical_not(home))
        def _():
            send(ze.at[xl], fx.at[c], f_s.at[1], f_r.at[c], at(c_=other))

    ready = {
        weights_on: (9, 11.8, 18.2, 20.3),
        partial: (14.7, 18.7, 22.5, 23.1),
        scatter: (16.2, 22.2, 24.6, 26.1),
        relay: (21.5, 26.4, 27.3, 30.3),
        activate: (25.2, 31.7, 32.9, 35),
        spread: (29.2, 36.6, 37.4, 38.1),
        gather: (34, 39.3, 41.2, 43),
        input_part: (35.6, 42, 43.2, 44.3),
        weight_part: (36.8, 42.4, 43.6, 45.1),
        weight_relay: (40.7, 45.7, 46.8, 49.6),
        weight_out: (45.5, 55, 56, 57),
    }
    late = {features: 5, features_done: 14.6, input_start: 44.5, input_relay: 51.6, input_near: 53}
    order = [(when, stage, None) for stage, when in late.items()]
    for stage, times in ready.items():
        shift = len(times) - n
        order += [(times[i if i < n - 1 else i + shift], stage, i) for i in range(n)]
    for _, stage, i in sorted(order, key=lambda entry: entry[0]):
        stage() if i is None else stage(i)

    @pl.when(jnp.logical_not(home))
    def _():
        arrived(fx.at[c], f_r.at[c])

    arrived(fx.at[other], f_r.at[other])
    for si in range(2):
        for cc in range(2):
            arrived(z_hub.at[si, cc], e_r.at[si, cc])
    for cc in range(2):
        got = fx[cc] + z_hub[0, cc].astype(F32) + z_hub[1, cc].astype(F32)
        for h in range(2):
            at_col = (2 * h + cc) * LANES
            dx_ref[:, at_col : at_col + LANES] = got[h * rows : (h + 1) * rows].astype(BF)

    @pl.when(home)
    def _():
        sent(xs.at[other], x_s.at[0])
        sent(window(other), gh_s)

    @pl.when(jnp.logical_not(home))
    def _():
        for cc in range(2):
            sent(part_of(xs.at[cc], turn), x_s.at[cc])
        sent(ze.at[xl], f_s.at[1])

    for copy in pending:
        copy.wait_send()


def store(a_ref, b_ref, c_ref, a_out, b_out, c_out, sem):
    pairs = ((a_ref, a_out), (b_ref, b_out), (c_ref, c_out))
    copies = [pltpu.make_async_copy(src, dst, sem.at[i]) for i, (src, dst) in enumerate(pairs)]
    for copy in copies:
        copy.start()
    for copy in copies:
        copy.wait()


def shards(ny, nz, inputs, grad_hidden, gate_weight, up_weight):
    tokens, features = inputs.shape
    columns = gate_weight.shape[1]
    cols = widths(columns)
    n = len(cols)
    share, rows = tokens // (2 * ny), tokens // nz
    yh, zh = ny // 4, nz // 4

    vmem = lambda shape, dtype=BF: pltpu.VMEM(shape, dtype)

    def ring(hops, block):
        return [
            (2, max(hops - 1, 1)) + block,
            (2, max(hops - 1, 1)) + block,
            block,
            (2,) + block,
            (2,) + block,
        ]

    z_block = (4 * rows, LANES)
    scratch = [
        vmem((2, 2, tokens, LANES)),
        vmem((2, 2, tokens, LANES)),
        vmem((4, LANES, tokens)),
        vmem((32, columns)),
        vmem((nz,) + z_block, F32),
        vmem((nz,) + z_block),
        vmem((2, 2 * rows, LANES), F32),
        vmem((2, 2 * rows, LANES), F32),
    ]
    z_ring = ring(zh, z_block)
    z_ring[3] = (2, 2, 2 * rows, LANES)
    scratch += [vmem(shape) for shape in z_ring]
    for shape, dtype in (
        (lambda w: (2, 4, LANES, w), BF),
        (lambda w: (2, ny, 2 * share, w), F32),
        (lambda w: (ny, 2 * share, w), F32),
        (lambda w: (ny, 2 * share, w), BF),
        (lambda w: (2, ny, 2 * share, w), BF),
        (lambda w: (4, 2, LANES, w), F32),
        (lambda w: (4, 2, LANES, w), BF),
        (lambda w: (6, LANES, w), BF),
        (lambda w: (2, LANES, w), BF),
    ):
        scratch += [vmem(shape(w), dtype) for w in cols]
    for j in range(5):
        scratch += [vmem(ring(yh, (2 * share, w))[j]) for w in cols]
    dma = pltpu.SemaphoreType.DMA
    scratch += [dma((2 * n + 4,)), dma((2,)), dma((2,)), dma((GROUP - 1,)), dma((GROUP - 1,))]
    scratch += [dma, dma, dma((2,)), dma((2,))]
    for shape in ((n, 4), (n,), (n, 4 * yh - 1), (n, ny - 1), (n,), (n, 6), (4 * zh - 1,)):
        scratch += [dma(shape), dma(shape)]
    scratch += [dma((2, 2)), dma((2, 2))]

    arrays = (inputs, grad_hidden, gate_weight, up_weight)
    in_hbm = pl.BlockSpec(memory_space=pl.ANY)
    in_vmem = pl.BlockSpec(memory_space=pltpu.VMEM)
    results = pl.pallas_call(
        functools.partial(kernel, ny, nz, cols),
        out_shape=(
            jax.ShapeDtypeStruct((rows, features), BF),
            jax.ShapeDtypeStruct(gate_weight.shape, BF),
            jax.ShapeDtypeStruct(up_weight.shape, BF),
        ),
        in_specs=[in_hbm] * 4,
        out_specs=(in_vmem,) * 3,
        scratch_shapes=scratch,
        compiler_params=pltpu.CompilerParams(
            collective_id=0, has_side_effects=True, vmem_limit_bytes=36 * 2**20
        ),
        name="step",
    )(*(pltpu.with_memory_space_constraint(a, pltpu.HBM) for a in arrays))
    return pl.pallas_call(
        store,
        out_shape=tuple(jax.ShapeDtypeStruct(r.shape, r.dtype) for r in results),
        in_specs=[pl.BlockSpec(memory_space=pl.ANY)] * 3,
        out_specs=(pl.BlockSpec(memory_space=pl.ANY),) * 3,
        scratch_shapes=[dma((3,))],
        name="store",
    )(*results)


def solution(mesh):
    placed = (
        P("dmod", "tok"),
        P("dmod", "hid"),
        P(("tok", "dmod"), "hid"),
        P(("tok", "dmod"), "hid"),
    )
    return jax.shard_map(
        functools.partial(shards, mesh.shape["tok"] // 2, mesh.shape["hid"]),
        mesh=mesh,
        in_specs=placed,
        out_specs=(P(("dmod", "hid"), "tok"), P(("tok", "dmod"), "hid"), P(("tok", "dmod"), "hid")),
        check_vma=False,
    )
```

```python
import functools

import jax
import jax.numpy as jnp
from jax import lax
from jax.experimental import pallas as pl
from jax.experimental.pallas import tpu as pltpu
from jax.sharding import PartitionSpec as P

BF, F32 = jnp.bfloat16, jnp.float32
LANES = 128
GROUP = 4
SIGNS = (1, -1)


def contract(a, b, dims):
    return lax.dot_general(a, b, (dims, ((), ())), preferred_element_type=F32)


def widths(columns):
    tiles = columns // LANES
    return [2 * LANES] * (tiles // 2) + [LANES] * (tiles % 2)


def kernel(ny, nz, cols, x_ref, gh_ref, wg_ref, wu_ref, dx_ref, dwg_ref, dwu_ref, *scratch):
    n = len(cols)
    starts = [sum(cols[:i]) for i in range(n)]
    it = iter(scratch)
    take = lambda count: [next(it) for _ in range(count)]
    xs, xg, xt, ghw, zf, zs, ze, fx = take(8)
    z_far, z_near, z_anti, z_hub, z_hubs = take(5)
    wb, pb, pr, ys, gb, dwf, dws, dwr, dwh = (take(n) for _ in range(9))
    y_far, y_near, y_anti, y_hub, y_hubs = (take(n) for _ in range(5))
    in_s, x_s, x_r, t_s, t_r, gh_s, gh_r, f_s, f_r = take(9)
    w_s, w_r, p_s, p_r, ys_s, ys_r, g_s, g_r, k_s, k_r, d_s, d_r, zs_s, zs_r, e_s, e_r = take(16)

    tok, dmod, z = lax.axis_index("tok"), lax.axis_index("dmod"), lax.axis_index("hid")
    xl, y, xh, c = tok // ny, tok % ny, dmod // 2, dmod % 2
    other = 1 - c
    x = dmod - c + xl
    q = 2 * xl + xh
    tokens = x_ref.shape[0]
    share = tokens // (2 * ny)
    rows = tokens // nz
    home = c == xl

    def at(xl_=xl, xh_=xh, y_=y, c_=c, z_=z):
        return {"tok": xl_ * ny + y_, "dmod": xh_ * 2 + c_, "hid": z_}

    def along_x(k):
        xk = (x + 4 + k) % 4
        return 2 * (xk % 2) + xk // 2, at(xl_=xk % 2, xh_=xk // 2)

    def along(axis, k):
        if axis == "y":
            return (y + ny + k) % ny
        return (z + nz + k) % nz

    def there(axis, k):
        return at(y_=along("y", k)) if axis == "y" else at(z_=along("z", k))

    def send(src, dst, send_sem, recv_sem, target):
        copy = pltpu.make_async_remote_copy(
            src_ref=src, dst_ref=dst, send_sem=send_sem, recv_sem=recv_sem,
            device_id=target, device_id_type=pl.DeviceIdType.MESH,
        )
        copy.start()
        return copy

    def arrived(dst, sem):
        pltpu.make_async_copy(dst, dst, sem).wait()

    sent = arrived
    pending = []

    barrier = pltpu.get_barrier_semaphore()
    y_hops, z_hops = ny // 4, nz // 4
    y_off = sorted({s * k % ny for k in range(1, y_hops + 1) for s in SIGNS})
    z_off = sorted({s * k % nz for k in range(1, max(z_hops, GROUP - 1) + 1) for s in SIGNS} - {0})
    peers = [at(c_=other), at(xl_=1 - xl, c_=other)] + [along_x(k)[1] for k in SIGNS]
    peers += [there("y", k) for k in y_off] + [there("z", k) for k in z_off]
    for k in sorted({s * z_hops % nz for s in SIGNS}):
        for a, b in ((xl, other), (1 - xl, c), (1 - xl, other)):
            peers.append(at(xl_=a, c_=b, z_=along("z", k)))
    for peer in peers[::-1]:
        pl.semaphore_signal(barrier, 1, device_id=peer, device_id_type=pl.DeviceIdType.MESH)

    local = []

    def bring(src, dst):
        copy = pltpu.make_async_copy(src, dst, in_s.at[len(local)])
        copy.start()
        local.append(copy)

    for i in range(n):
        span = pl.ds(starts[i], cols[i])
        bring(wg_ref.at[:, span], wb[i].at[0, q])
        bring(wu_ref.at[:, span], wb[i].at[1, q])
    for h in range(2):
        for cc in range(2):
            bring(x_ref.at[:, pl.ds((2 * h + cc) * LANES, LANES)], xs.at[cc, h])

    def window(core):
        turn = core * ny + y
        first = pl.multiple_of(2 * share * (turn // 2) + 16 * (turn % 2), 16)
        return gh_ref.at[pl.ds(first, 32), :]

    own_gh = pltpu.make_async_copy(window(c), ghw, gh_r)

    @pl.when(home)
    def _():
        own_gh.start()

    for copy in local:
        copy.wait()

    @pl.when(home)
    def _():
        xg[xl] = xs[c]

    pl.semaphore_wait(barrier, len(peers))

    def weights_out(i):
        own = wb[i].at[:, q]
        for slot, k in enumerate(SIGNS):
            pending.append(send(own, own, w_s.at[i, slot], w_r.at[i, slot], along_x(k)[1]))

    part = tokens // GROUP
    turn = z % GROUP

    def part_of(slab, j):
        return slab.at[:, pl.ds(pl.multiple_of(j * part, part), part)]

    to_core = (xs.at[other], xg.at[xl], x_s.at[0], x_r.at[0], at(c_=other))
    to_gh = (window(other), ghw, gh_s, gh_r, at(c_=other))
    to_chip = [
        (part_of(xs.at[cc], turn), part_of(xg.at[xl], turn), x_s.at[cc], x_r.at[1],
         at(xl_=1 - xl, c_=cc))
        for cc in range(2)
    ]

    @pl.when(home)
    def _():
        send(*to_core)
        send(*to_gh)

    @pl.when(jnp.logical_not(home))
    def _():
        for args in to_chip:
            send(*args)

    weights_out(0)
    weights_out(1)

    def features():
        mine = part_of(xg.at[1 - xl], turn)
        arrived(mine, x_r.at[1])
        for k in range(1, GROUP):
            mate = z - turn + (turn + k) % GROUP
            pending.append(send(mine, mine, t_s.at[k - 1], t_r.at[k - 1], at(z_=mate)))

    def features_done():
        for k in range(1, GROUP):
            arrived(part_of(xg.at[1 - xl], (turn + GROUP - k) % GROUP), t_r.at[k - 1])

        @pl.when(jnp.logical_not(home))
        def _():
            arrived(xg.at[xl], x_r.at[0])

        for b in range(4):
            xt[b] = xg[b // 2, b % 2].astype(F32).T.astype(BF)

    def weights_on(i):
        for slot, k in enumerate(SIGNS):
            qk = along_x(-k)[0]
            arrived(wb[i].at[:, qk], w_r.at[i, slot])
            block = wb[i].at[slot, qk]
            pending.append(
                send(block, block, w_s.at[i, 2 + slot], w_r.at[i, 2 + slot], along_x(k)[1])
            )
        if i + 2 < n:
            weights_out(i + 2)

    def partial(i):
        qk = along_x(2)[0]
        for slot in range(2):
            arrived(wb[i].at[slot, qk], w_r.at[i, 2 + slot])
        wide = jnp.concatenate([xg[b // 2, b % 2] for b in range(4)], axis=1)
        for m in range(2):
            w = wb[i][m].reshape(4 * LANES, cols[i])
            block = contract(wide, w, ((1,), (0,))).reshape(2, ny, share, cols[i])
            pb[i][:, :, m * share : (m + 1) * share] = block
        pending.append(send(pb[i].at[other], pr[i], p_s.at[i], p_r.at[i], at(c_=other)))

    def reduce_start(axis, hops, src, far, near, anti, s_sem, r_sem):
        pick = lambda k: src.at[along(axis, k)]
        way = 2 * (along(axis, 0) % 2) - 1
        for j in range(hops - 1, 0, -1):
            for si, s in enumerate(SIGNS):
                slot = si * (hops - 1) + j - 1
                pending.append(
                    send(pick(s * (j + hops)), far.at[si, j - 1], s_sem.at[slot], r_sem.at[slot],
                         there(axis, s * j))
                )
        slot = 2 * (hops - 1)
        pending.append(
            send(pick(2 * hops), anti, s_sem.at[slot], r_sem.at[slot], there(axis, way * hops))
        )
        for j in range(1, hops):
            for si, s in enumerate(SIGNS):
                slot = (2 + si) * (hops - 1) + j
                pending.append(
                    send(pick(s * j), near.at[si, j - 1], s_sem.at[slot], r_sem.at[slot],
                         there(axis, s * j))
                )

    def reduce_relay(axis, hops, own, far, anti, hubs, r_sem, deliver):
        odd = along(axis, 0) % 2
        for j in range(1, hops):
            for si in range(2):
                arrived(far.at[si, j - 1], r_sem.at[si * (hops - 1) + j - 1])
        arrived(anti, r_sem.at[2 * (hops - 1)])
        for first in (True, False):
            si = 1 - odd if first else odd
            way = 1 - 2 * si
            total = own(along(axis, way * hops))
            for j in range(1, hops):
                total = total + far[si, j - 1].astype(F32)
            if first:
                total = total + anti[...].astype(F32)
            hubs[si] = total.astype(BF)
            deliver(si, along(axis, way * hops))

    def reduce_near(axis, hops, own, near, r_sem):
        total = own(along(axis, 0))
        for j in range(1, hops):
            for si in range(2):
                arrived(near.at[si, j - 1], r_sem.at[(2 + si) * (hops - 1) + j])
                total = total + near[si, j - 1].astype(F32)
        return total

    def own_sum(i):
        return lambda yk: pb[i][c, yk] + pr[i][yk]

    def scatter(i):
        arrived(pr[i], p_r.at[i])
        ys[i][...] = (pb[i][c] + pr[i][...]).astype(BF)
        reduce_start("y", y_hops, ys[i], y_far[i], y_near[i], y_anti[i], ys_s.at[i], ys_r.at[i])

    y_slot = 4 * (y_hops - 1) + 1

    def relay(i):
        def deliver(si, yk):
            src, slot = y_hubs[i].at[si], y_slot + si
            pending.append(
                send(src, y_hub[i].at[si], ys_s.at[i, slot], ys_r.at[i, slot], at(y_=yk))
            )

        reduce_relay("y", y_hops, own_sum(i), y_far[i], y_anti[i], y_hubs[i], ys_r.at[i], deliver)

    def activate(i):
        if i == 0:
            @pl.when(home)
            def _():
                own_gh.wait()

            @pl.when(jnp.logical_not(home))
            def _():
                arrived(ghw, gh_r)

        total = reduce_near("y", y_hops, own_sum(i), y_near[i], ys_r.at[i])
        for si in range(2):
            arrived(y_hub[i].at[si], ys_r.at[i, y_slot + si])
            total = total + y_hub[i][si].astype(F32)
        gate, up = total[:share], total[share:]
        upstream = ghw[:, starts[i] : starts[i] + cols[i]].astype(F32)
        upstream = jnp.where((c * ny + y) % 2 == 1, upstream[8 : 8 + share], upstream[:share])
        sigma = jax.nn.sigmoid(gate)
        grad_gate = upstream * up * sigma * (1.0 + gate * (1.0 - sigma))
        grad_up = upstream * gate * sigma
        gb[i][c, y] = jnp.concatenate([grad_gate, grad_up], axis=0).astype(BF)
        own = gb[i].at[c, y]
        for k in range(y_hops, 0, -1):
            for s in SIGNS:
                slot = s * k % ny - 1
                pending.append(send(own, own, g_s.at[i, slot], g_r.at[i, slot], there("y", s * k)))

    def spread(i):
        for s in SIGNS:
            block = gb[i].at[c, along("y", -s * y_hops)]
            arrived(block, g_r.at[i, s * y_hops % ny - 1])
            for j in range(1, y_hops):
                slot = s * (j + y_hops) % ny - 1
                pending.append(send(block, block, g_s.at[i, slot], g_r.at[i, slot], there("y", s * j)))
        way = 2 * (y % 2) - 1
        block = gb[i].at[c, along("y", -way * y_hops)]
        slot = 2 * y_hops - 1
        pending.append(
            send(block, block, g_s.at[i, slot], g_r.at[i, slot], there("y", way * y_hops))
        )

    def gather(i):
        for k in range(1, ny):
            if k not in (y_hops, ny - y_hops):
                arrived(gb[i].at[c, along("y", -k)], g_r.at[i, k - 1])
        pending.append(send(gb[i].at[c], gb[i].at[c], k_s.at[i], k_r.at[i], at(c_=other)))

    def grads_of(i):
        both = gb[i][...].astype(F32).reshape(2 * ny, 2 * share, cols[i])
        grad_gate = both[:, :share].reshape(tokens, cols[i]).astype(BF)
        grad_up = both[:, share:].reshape(tokens, cols[i]).astype(BF)
        return grad_gate, grad_up

    def input_part(i):
        arrived(gb[i].at[other], k_r.at[i])
        grads = grads_of(i)
        for b in range(4):
            total = 0.0
            for m, grad in enumerate(grads):
                total = total + contract(grad, wb[i][m, b], ((1,), (1,)))
            total = total.reshape(nz, rows, LANES)
            span = slice(b * rows, (b + 1) * rows)
            zf[:, span] = total if i == 0 else zf[:, span] + total

    def weight_part(i):
        for m, grad in enumerate(grads_of(i)):
            for b in range(4):
                dwf[i][b, m] = contract(xt[b], grad, ((1,), (0,)))
        dws[i][...] = dwf[i][...].astype(BF)
        q2 = along_x(2)[0]
        for m, k in enumerate(SIGNS):
            pending.append(
                send(dws[i].at[q2, m], dwr[i].at[m], d_s.at[i, m], d_r.at[i, m], along_x(k)[1])
            )
        for m, k in enumerate(SIGNS):
            qk, target = along_x(k)
            pending.append(
                send(dws[i].at[qk, 1 - m], dwr[i].at[2 + m], d_s.at[i, 2 + m], d_r.at[i, 2 + m], target)
            )

    def weight_relay(i):
        for m, k in enumerate(SIGNS):
            qk, target = along_x(k)
            arrived(dwr[i].at[m], d_r.at[i, m])
            dwh[i][m] = (dwf[i][qk, m] + dwr[i][m].astype(F32)).astype(BF)
            pending.append(
                send(dwh[i].at[m], dwr[i].at[4 + m], d_s.at[i, 4 + m], d_r.at[i, 4 + m], target)
            )

    def weight_out(i):
        span = slice(starts[i], starts[i] + cols[i])
        for m, out in enumerate((dwg_ref, dwu_ref)):
            total = dwf[i][q, m]
            for slot in (3 - m, 4 + m):
                arrived(dwr[i].at[slot], d_r.at[i, slot])
                total = total + dwr[i][slot].astype(F32)
            out[:, span] = total.astype(BF)

    own_input = lambda zk: zf[zk]

    def input_start():
        zs[...] = zf[...].astype(BF)
        reduce_start("z", z_hops, zs, z_far, z_near, z_anti, zs_s, zs_r)

    half = 2 * rows

    def input_relay():
        def deliver(si, zk):
            for to in range(2):
                target = at(xl_=to, c_=xl, z_=zk)
                src = z_hubs.at[si, pl.ds(to * half, half)]
                pending.append(send(src, z_hub.at[si, c], e_s.at[si, to], e_r.at[si, c], target))

        reduce_relay("z", z_hops, own_input, z_far, z_anti, z_hubs, zs_r, deliver)

    def input_near():
        total = reduce_near("z", z_hops, own_input, z_near, zs_r)
        ze[...] = total.reshape(2, half, LANES)
        target = at(xl_=1 - xl, c_=xl)
        pending.append(send(ze.at[1 - xl], fx.at[c], f_s.at[0], f_r.at[c], target))

        @pl.when(home)
        def _():
            fx[c] = ze[xl]

        @pl.when(jnp.logical_not(home))
        def _():
            send(ze.at[xl], fx.at[c], f_s.at[1], f_r.at[c], at(c_=other))

    ready = {
        weights_on: (9, 11.8, 18.2, 20.3),
        partial: (14.7, 18.7, 22.5, 23.1),
        scatter: (16.2, 22.2, 24.6, 26.1),
        relay: (21.5, 26.4, 27.3, 30.3),
        activate: (25.2, 31.7, 32.9, 35),
        spread: (29.2, 36.6, 37.4, 38.1),
        gather: (34, 39.3, 41.2, 43),
        input_part: (35.6, 42, 43.2, 44.3),
        weight_part: (36.8, 42.4, 43.6, 45.1),
        weight_relay: (40.7, 45.7, 46.8, 49.6),
        weight_out: (45.5, 55, 56, 57),
    }
    late = {features: 5, features_done: 14.6, input_start: 44.5, input_relay: 51.6, input_near: 53}
    order = [(when, stage, None) for stage, when in late.items()]
    for stage, times in ready.items():
        shift = len(times) - n
        order += [(times[i if i < n - 1 else i + shift], stage, i) for i in range(n)]
    for _, stage, i in sorted(order, key=lambda entry: entry[0]):
        stage() if i is None else stage(i)

    @pl.when(jnp.logical_not(home))
    def _():
        arrived(fx.at[c], f_r.at[c])

    arrived(fx.at[other], f_r.at[other])
    for si in range(2):
        for cc in range(2):
            arrived(z_hub.at[si, cc], e_r.at[si, cc])
    for cc in range(2):
        got = fx[cc] + z_hub[0, cc].astype(F32) + z_hub[1, cc].astype(F32)
        for h in range(2):
            at_col = (2 * h + cc) * LANES
            dx_ref[:, at_col : at_col + LANES] = got[h * rows : (h + 1) * rows].astype(BF)

    @pl.when(home)
    def _():
        sent(xs.at[other], x_s.at[0])
        sent(window(other), gh_s)

    @pl.when(jnp.logical_not(home))
    def _():
        for cc in range(2):
            sent(part_of(xs.at[cc], turn), x_s.at[cc])
        sent(ze.at[xl], f_s.at[1])

    for copy in pending:
        copy.wait_send()


def shards(ny, nz, inputs, grad_hidden, gate_weight, up_weight):
    tokens, features = inputs.shape
    columns = gate_weight.shape[1]
    cols = widths(columns)
    n = len(cols)
    share, rows = tokens // (2 * ny), tokens // nz
    yh, zh = ny // 4, nz // 4

    vmem = lambda shape, dtype=BF: pltpu.VMEM(shape, dtype)

    def ring(hops, block):
        return [
            (2, max(hops - 1, 1)) + block,
            (2, max(hops - 1, 1)) + block,
            block,
            (2,) + block,
            (2,) + block,
        ]

    z_block = (4 * rows, LANES)
    scratch = [
        vmem((2, 2, tokens, LANES)),
        vmem((2, 2, tokens, LANES)),
        vmem((4, LANES, tokens)),
        vmem((32, columns)),
        vmem((nz,) + z_block, F32),
        vmem((nz,) + z_block),
        vmem((2, 2 * rows, LANES), F32),
        vmem((2, 2 * rows, LANES), F32),
    ]
    z_ring = ring(zh, z_block)
    z_ring[3] = (2, 2, 2 * rows, LANES)
    scratch += [vmem(shape) for shape in z_ring]
    for shape, dtype in (
        (lambda w: (2, 4, LANES, w), BF),
        (lambda w: (2, ny, 2 * share, w), F32),
        (lambda w: (ny, 2 * share, w), F32),
        (lambda w: (ny, 2 * share, w), BF),
        (lambda w: (2, ny, 2 * share, w), BF),
        (lambda w: (4, 2, LANES, w), F32),
        (lambda w: (4, 2, LANES, w), BF),
        (lambda w: (6, LANES, w), BF),
        (lambda w: (2, LANES, w), BF),
    ):
        scratch += [vmem(shape(w), dtype) for w in cols]
    for j in range(5):
        scratch += [vmem(ring(yh, (2 * share, w))[j]) for w in cols]
    dma = pltpu.SemaphoreType.DMA
    scratch += [dma((2 * n + 4,)), dma((2,)), dma((2,)), dma((GROUP - 1,)), dma((GROUP - 1,))]
    scratch += [dma, dma, dma((2,)), dma((2,))]
    for shape in ((n, 4), (n,), (n, 4 * yh - 1), (n, ny - 1), (n,), (n, 6), (4 * zh - 1,)):
        scratch += [dma(shape), dma(shape)]
    scratch += [dma((2, 2)), dma((2, 2))]

    arrays = (inputs, grad_hidden, gate_weight, up_weight)
    in_hbm = pl.BlockSpec(memory_space=pl.ANY)
    in_vmem = pl.BlockSpec(memory_space=pltpu.VMEM)
    return pl.pallas_call(
        functools.partial(kernel, ny, nz, cols),
        out_shape=(
            jax.ShapeDtypeStruct((rows, features), BF),
            jax.ShapeDtypeStruct(gate_weight.shape, BF),
            jax.ShapeDtypeStruct(up_weight.shape, BF),
        ),
        in_specs=[in_hbm] * 4,
        out_specs=(in_vmem,) * 3,
        scratch_shapes=scratch,
        compiler_params=pltpu.CompilerParams(
            collective_id=0, has_side_effects=True, vmem_limit_bytes=36 * 2**20
        ),
        name="step",
    )(*(pltpu.with_memory_space_constraint(a, pltpu.HBM) for a in arrays))


def solution(mesh):
    placed = (
        P("dmod", "tok"),
        P("dmod", "hid"),
        P(("tok", "dmod"), "hid"),
        P(("tok", "dmod"), "hid"),
    )
    return jax.shard_map(
        functools.partial(shards, mesh.shape["tok"] // 2, mesh.shape["hid"]),
        mesh=mesh,
        in_specs=placed,
        out_specs=(P(("dmod", "hid"), "tok"), P(("tok", "dmod"), "hid"), P(("tok", "dmod"), "hid")),
        check_vma=False,
    )
```

```python
import functools

import jax
import jax.numpy as jnp
from jax import lax
from jax.experimental import pallas as pl
from jax.experimental.pallas import tpu as pltpu
from jax.sharding import PartitionSpec as P

BF, F32 = jnp.bfloat16, jnp.float32
LANES = 128
GROUP = 4
SIGNS = (1, -1)


def contract(a, b, dims):
    return lax.dot_general(a, b, (dims, ((), ())), preferred_element_type=F32)


def widths(columns):
    tiles = columns // LANES
    return [2 * LANES] * (tiles // 2) + [LANES] * (tiles % 2)


def kernel(ny, nz, cols, x_ref, gh_ref, wg_ref, wu_ref, dx_ref, dw_ref, *scratch):
    n = len(cols)
    starts = [sum(cols[:i]) for i in range(n)]
    it = iter(scratch)
    take = lambda count: [next(it) for _ in range(count)]
    xs, xg, xt, ghw, zf, zs, ze, fx = take(8)
    z_far, z_near, z_anti, z_hub, z_hubs = take(5)
    wb, pb, pr, ys, gb, dwf, dws, dwr, dwh = (take(n) for _ in range(9))
    y_far, y_near, y_anti, y_hub, y_hubs = (take(n) for _ in range(5))
    in_s, x_s, x_r, t_s, t_r, gh_s, gh_r, f_s, f_r = take(9)
    w_s, w_r, p_s, p_r, ys_s, ys_r, g_s, g_r, k_s, k_r, d_s, d_r, zs_s, zs_r, e_s, e_r = take(16)

    tok, dmod, z = lax.axis_index("tok"), lax.axis_index("dmod"), lax.axis_index("hid")
    xl, y, xh, c = tok // ny, tok % ny, dmod // 2, dmod % 2
    other = 1 - c
    x = dmod - c + xl
    q = 2 * xl + xh
    tokens = x_ref.shape[0]
    share = tokens // (2 * ny)
    rows = tokens // nz
    home = c == xl

    def at(xl_=xl, xh_=xh, y_=y, c_=c, z_=z):
        return {"tok": xl_ * ny + y_, "dmod": xh_ * 2 + c_, "hid": z_}

    def along_x(k):
        xk = (x + 4 + k) % 4
        return 2 * (xk % 2) + xk // 2, at(xl_=xk % 2, xh_=xk // 2)

    def along(axis, k):
        if axis == "y":
            return (y + ny + k) % ny
        return (z + nz + k) % nz

    def there(axis, k):
        return at(y_=along("y", k)) if axis == "y" else at(z_=along("z", k))

    def send(src, dst, send_sem, recv_sem, target):
        copy = pltpu.make_async_remote_copy(
            src_ref=src, dst_ref=dst, send_sem=send_sem, recv_sem=recv_sem,
            device_id=target, device_id_type=pl.DeviceIdType.MESH,
        )
        copy.start()
        return copy

    def arrived(dst, sem):
        pltpu.make_async_copy(dst, dst, sem).wait()

    sent = arrived
    pending = []

    barrier = pltpu.get_barrier_semaphore()
    y_hops, z_hops = ny // 4, nz // 4
    y_off = sorted({s * k % ny for k in range(1, y_hops + 1) for s in SIGNS})
    z_off = sorted({s * k % nz for k in range(1, max(z_hops, GROUP - 1) + 1) for s in SIGNS} - {0})
    peers = [at(c_=other), at(xl_=1 - xl, c_=other)] + [along_x(k)[1] for k in SIGNS]
    peers += [there("y", k) for k in y_off] + [there("z", k) for k in z_off]
    for k in sorted({s * z_hops % nz for s in SIGNS}):
        for a, b in ((xl, other), (1 - xl, c), (1 - xl, other)):
            peers.append(at(xl_=a, c_=b, z_=along("z", k)))
    local = []

    def bring(src, dst):
        copy = pltpu.make_async_copy(src, dst, in_s.at[len(local)])
        copy.start()
        local.append(copy)

    def bring_weights(i):
        span = pl.ds(starts[i], cols[i])
        bring(wg_ref.at[:, span], wb[i].at[0, q])
        bring(wu_ref.at[:, span], wb[i].at[1, q])

    bring_weights(0)
    for h in range(2):
        for cc in range(2):
            bring(x_ref.at[:, pl.ds((2 * h + cc) * LANES, LANES)], xs.at[cc, h])
    first_in = len(local)
    for peer in peers[::-1]:
        pl.semaphore_signal(barrier, 1, device_id=peer, device_id_type=pl.DeviceIdType.MESH)
    for i in range(1, n):
        bring_weights(i)

    def window(core):
        turn = core * ny + y
        first = pl.multiple_of(2 * share * (turn // 2) + 16 * (turn % 2), 16)
        return gh_ref.at[pl.ds(first, 32), :]

    own_gh = pltpu.make_async_copy(window(c), ghw, gh_r)

    @pl.when(home)
    def _():
        own_gh.start()

    for copy in local[:first_in]:
        copy.wait()

    @pl.when(home)
    def _():
        xg[xl] = xs[c]

    pl.semaphore_wait(barrier, len(peers))

    def weights_out(i):
        own = wb[i].at[:, q]
        for slot, k in enumerate(SIGNS):
            pending.append(send(own, own, w_s.at[i, slot], w_r.at[i, slot], along_x(k)[1]))

    part = tokens // GROUP
    turn = z % GROUP

    def part_of(slab, j):
        return slab.at[:, pl.ds(pl.multiple_of(j * part, part), part)]

    to_core = (xs.at[other], xg.at[xl], x_s.at[0], x_r.at[0], at(c_=other))
    to_gh = (window(other), ghw, gh_s, gh_r, at(c_=other))
    to_chip = [
        (part_of(xs.at[cc], turn), part_of(xg.at[xl], turn), x_s.at[cc], x_r.at[1],
         at(xl_=1 - xl, c_=cc))
        for cc in range(2)
    ]

    @pl.when(home)
    def _():
        send(*to_core)
        send(*to_gh)

    @pl.when(jnp.logical_not(home))
    def _():
        for args in to_chip:
            send(*args)

    weights_out(0)
    for copy in local[first_in:]:
        copy.wait()
    weights_out(1)

    def features():
        mine = part_of(xg.at[1 - xl], turn)
        arrived(mine, x_r.at[1])
        for k in range(1, GROUP):
            mate = z - turn + (turn + k) % GROUP
            pending.append(send(mine, mine, t_s.at[k - 1], t_r.at[k - 1], at(z_=mate)))

    def features_done():
        for k in range(1, GROUP):
            arrived(part_of(xg.at[1 - xl], (turn + GROUP - k) % GROUP), t_r.at[k - 1])

        @pl.when(jnp.logical_not(home))
        def _():
            arrived(xg.at[xl], x_r.at[0])

        for b in range(4):
            xt[b] = xg[b // 2, b % 2].astype(F32).T.astype(BF)

    def weights_on(i):
        for slot, k in enumerate(SIGNS):
            qk = along_x(-k)[0]
            arrived(wb[i].at[:, qk], w_r.at[i, slot])
            block = wb[i].at[slot, qk]
            pending.append(
                send(block, block, w_s.at[i, 2 + slot], w_r.at[i, 2 + slot], along_x(k)[1])
            )
        if i + 2 < n:
            weights_out(i + 2)

    def partial(i):
        qk = along_x(2)[0]
        for slot in range(2):
            arrived(wb[i].at[slot, qk], w_r.at[i, 2 + slot])
        wide = jnp.concatenate([xg[b // 2, b % 2] for b in range(4)], axis=1)
        for m in range(2):
            w = wb[i][m].reshape(4 * LANES, cols[i])
            block = contract(wide, w, ((1,), (0,))).reshape(2, ny, share, cols[i])
            pb[i][:, :, m * share : (m + 1) * share] = block
        pending.append(send(pb[i].at[other], pr[i], p_s.at[i], p_r.at[i], at(c_=other)))

    def reduce_start(axis, hops, src, far, near, anti, s_sem, r_sem, cuts=1):
        place = lambda k: along(axis, k)
        way = 2 * (along(axis, 0) % 2) - 1
        lines = src.shape[1] // cuts
        for cut in range(cuts):
            part = pl.ds(cut * lines, lines)
            for j in range(hops - 1, 0, -1):
                for si, s in enumerate(SIGNS):
                    slot = (si * (hops - 1) + j - 1) * cuts + cut
                    pending.append(
                        send(src.at[place(s * (j + hops)), part], far.at[si, j - 1, part],
                             s_sem.at[slot], r_sem.at[slot], there(axis, s * j))
                    )
            slot = 2 * (hops - 1) * cuts + cut
            pending.append(
                send(src.at[place(2 * hops), part], anti.at[part], s_sem.at[slot], r_sem.at[slot],
                     there(axis, way * hops))
            )
        for j in range(1, hops):
            for si, s in enumerate(SIGNS):
                slot = (2 * hops - 1) * cuts + si * (hops - 1) + j - 1
                pending.append(
                    send(src.at[place(s * j)], near.at[si, j - 1], s_sem.at[slot], r_sem.at[slot],
                         there(axis, s * j))
                )

    def reduce_relay(axis, hops, own, far, anti, hubs, r_sem, deliver, cut=0, cuts=1):
        odd = along(axis, 0) % 2
        lines = hubs.shape[1] // cuts
        part = pl.ds(cut * lines, lines)
        for j in range(1, hops):
            for si in range(2):
                slot = (si * (hops - 1) + j - 1) * cuts + cut
                arrived(far.at[si, j - 1, part], r_sem.at[slot])
        arrived(anti.at[part], r_sem.at[2 * (hops - 1) * cuts + cut])
        for first in (True, False):
            si = 1 - odd if first else odd
            way = 1 - 2 * si
            total = own(along(axis, way * hops), part)
            for j in range(1, hops):
                total = total + far[si, j - 1, part].astype(F32)
            if first:
                total = total + anti[part].astype(F32)
            hubs[si, part] = total.astype(BF)
            deliver(si, along(axis, way * hops))

    def reduce_near(axis, hops, own, near, r_sem, cuts=1):
        total = own(along(axis, 0), slice(None))
        for j in range(1, hops):
            for si in range(2):
                slot = (2 * hops - 1) * cuts + si * (hops - 1) + j - 1
                arrived(near.at[si, j - 1], r_sem.at[slot])
                total = total + near[si, j - 1].astype(F32)
        return total

    def own_sum(i):
        return lambda yk, part: pb[i][c, yk, part] + pr[i][yk, part]

    def scatter(i):
        arrived(pr[i], p_r.at[i])
        ys[i][...] = (pb[i][c] + pr[i][...]).astype(BF)
        reduce_start("y", y_hops, ys[i], y_far[i], y_near[i], y_anti[i], ys_s.at[i], ys_r.at[i])

    y_slot = 4 * (y_hops - 1) + 1

    def relay(i):
        def deliver(si, yk):
            src, slot = y_hubs[i].at[si], y_slot + si
            pending.append(
                send(src, y_hub[i].at[si], ys_s.at[i, slot], ys_r.at[i, slot], at(y_=yk))
            )

        reduce_relay("y", y_hops, own_sum(i), y_far[i], y_anti[i], y_hubs[i], ys_r.at[i], deliver)

    def activate(i):
        if i == 0:
            @pl.when(home)
            def _():
                own_gh.wait()

            @pl.when(jnp.logical_not(home))
            def _():
                arrived(ghw, gh_r)

        total = reduce_near("y", y_hops, own_sum(i), y_near[i], ys_r.at[i])
        for si in range(2):
            arrived(y_hub[i].at[si], ys_r.at[i, y_slot + si])
            total = total + y_hub[i][si].astype(F32)
        gate, up = total[:share], total[share:]
        upstream = ghw[:, starts[i] : starts[i] + cols[i]].astype(F32)
        upstream = jnp.where((c * ny + y) % 2 == 1, upstream[8 : 8 + share], upstream[:share])
        sigma = jax.nn.sigmoid(gate)
        grad_gate = upstream * up * sigma * (1.0 + gate * (1.0 - sigma))
        grad_up = upstream * gate * sigma
        gb[i][c, y] = jnp.concatenate([grad_gate, grad_up], axis=0).astype(BF)
        own = gb[i].at[c, y]
        for k in range(y_hops, 0, -1):
            for s in SIGNS:
                slot = s * k % ny - 1
                pending.append(send(own, own, g_s.at[i, slot], g_r.at[i, slot], there("y", s * k)))

    def spread(i):
        for s in SIGNS:
            block = gb[i].at[c, along("y", -s * y_hops)]
            arrived(block, g_r.at[i, s * y_hops % ny - 1])
            for j in range(1, y_hops):
                slot = s * (j + y_hops) % ny - 1
                pending.append(send(block, block, g_s.at[i, slot], g_r.at[i, slot], there("y", s * j)))
        way = 2 * (y % 2) - 1
        block = gb[i].at[c, along("y", -way * y_hops)]
        slot = 2 * y_hops - 1
        pending.append(
            send(block, block, g_s.at[i, slot], g_r.at[i, slot], there("y", way * y_hops))
        )

    def gather(i):
        for k in range(1, ny):
            if k not in (y_hops, ny - y_hops):
                arrived(gb[i].at[c, along("y", -k)], g_r.at[i, k - 1])
        pending.append(send(gb[i].at[c], gb[i].at[c], k_s.at[i], k_r.at[i], at(c_=other)))

    def grads_of(i):
        both = gb[i][...].astype(F32).reshape(2 * ny, 2 * share, cols[i])
        grad_gate = both[:, :share].reshape(tokens, cols[i]).astype(BF)
        grad_up = both[:, share:].reshape(tokens, cols[i]).astype(BF)
        return grad_gate, grad_up

    def input_part(i):
        arrived(gb[i].at[other], k_r.at[i])
        grads = grads_of(i)
        for b in range(4):
            total = 0.0
            for m, grad in enumerate(grads):
                total = total + contract(grad, wb[i][m, b], ((1,), (1,)))
            total = total.reshape(nz, rows, LANES)
            span = slice(b * rows, (b + 1) * rows)
            zf[:, span] = total if i == 0 else zf[:, span] + total

    def weight_part(i):
        for m, grad in enumerate(grads_of(i)):
            for b in range(4):
                dwf[i][b, m] = contract(xt[b], grad, ((1,), (0,)))
        dws[i][...] = dwf[i][...].astype(BF)
        q2 = along_x(2)[0]
        for m, k in enumerate(SIGNS):
            pending.append(
                send(dws[i].at[q2, m], dwr[i].at[m], d_s.at[i, m], d_r.at[i, m], along_x(k)[1])
            )
        for m, k in enumerate(SIGNS):
            qk, target = along_x(k)
            pending.append(
                send(dws[i].at[qk, 1 - m], dwr[i].at[2 + m], d_s.at[i, 2 + m], d_r.at[i, 2 + m], target)
            )

    def weight_relay(i):
        for m, k in enumerate(SIGNS):
            qk, target = along_x(k)
            arrived(dwr[i].at[m], d_r.at[i, m])
            dwh[i][m] = (dwf[i][qk, m] + dwr[i][m].astype(F32)).astype(BF)
            pending.append(
                send(dwh[i].at[m], dwr[i].at[4 + m], d_s.at[i, 4 + m], d_r.at[i, 4 + m], target)
            )

    def weight_out(i):
        span = slice(starts[i], starts[i] + cols[i])
        for m in range(2):
            total = dwf[i][q, m]
            for slot in (3 - m, 4 + m):
                arrived(dwr[i].at[slot], d_r.at[i, slot])
                total = total + dwr[i][slot].astype(F32)
            dw_ref[m, :, span] = total.astype(BF)

    own_input = lambda zk, part: zf[zk, part]

    def input_start():
        zs[...] = zf[...].astype(BF)
        reduce_start("z", z_hops, zs, z_far, z_near, z_anti, zs_s, zs_r, 2)

    half = 2 * rows

    def input_relay(to):
        def deliver(si, zk):
            target = at(xl_=to, c_=xl, z_=zk)
            src = z_hubs.at[si, pl.ds(to * half, half)]
            pending.append(send(src, z_hub.at[si, c], e_s.at[si, to], e_r.at[si, c], target))

        reduce_relay("z", z_hops, own_input, z_far, z_anti, z_hubs, zs_r, deliver, to, 2)

    def input_near():
        total = reduce_near("z", z_hops, own_input, z_near, zs_r, 2)
        ze[...] = total.reshape(2, half, LANES)
        target = at(xl_=1 - xl, c_=xl)
        pending.append(send(ze.at[1 - xl], fx.at[c], f_s.at[0], f_r.at[c], target))

        @pl.when(home)
        def _():
            fx[c] = ze[xl]

        @pl.when(jnp.logical_not(home))
        def _():
            send(ze.at[xl], fx.at[c], f_s.at[1], f_r.at[c], at(c_=other))

    ready = {
        weights_on: (9, 11.8, 18.2, 20.3),
        partial: (14.7, 18.7, 22.5, 23.1),
        scatter: (16.2, 22.2, 24.6, 26.1),
        relay: (21.5, 26.4, 27.3, 30.3),
        activate: (25.2, 31.7, 32.9, 35),
        spread: (29.2, 36.6, 37.4, 38.1),
        gather: (34, 39.3, 41.2, 43),
        input_part: (35.6, 42, 43.2, 44.3),
        weight_part: (36.8, 42.4, 43.6, 45.1),
        weight_relay: (40.7, 45.7, 46.8, 49.6),
        weight_out: (45.5, 55, 56, 57),
    }
    late = {features: 5, features_done: 14.6, input_start: 44.5, input_near: 53}
    order = [(when, stage, None) for stage, when in late.items()]
    order += [(48.5, input_relay, 0), (51.6, input_relay, 1)]
    for stage, times in ready.items():
        shift = len(times) - n
        order += [(times[i if i < n - 1 else i + shift], stage, i) for i in range(n)]
    for _, stage, i in sorted(order, key=lambda entry: entry[0]):
        stage() if i is None else stage(i)

    recent = 24
    for copy in pending[:-recent]:
        copy.wait_send()

    @pl.when(home)
    def _():
        sent(xs.at[other], x_s.at[0])
        sent(window(other), gh_s)

    @pl.when(jnp.logical_not(home))
    def _():
        for cc in range(2):
            sent(part_of(xs.at[cc], turn), x_s.at[cc])

    @pl.when(jnp.logical_not(home))
    def _():
        arrived(fx.at[c], f_r.at[c])

    arrived(fx.at[other], f_r.at[other])
    for si in range(2):
        for cc in range(2):
            arrived(z_hub.at[si, cc], e_r.at[si, cc])
    for cc in range(2):
        got = fx[cc] + z_hub[0, cc].astype(F32) + z_hub[1, cc].astype(F32)
        for h in range(2):
            at_col = (2 * h + cc) * LANES
            dx_ref[:, at_col : at_col + LANES] = got[h * rows : (h + 1) * rows].astype(BF)

    @pl.when(jnp.logical_not(home))
    def _():
        sent(ze.at[xl], f_s.at[1])

    for copy in pending[-recent:]:
        copy.wait_send()


def shards(ny, nz, inputs, grad_hidden, gate_weight, up_weight):
    tokens, features = inputs.shape
    columns = gate_weight.shape[1]
    cols = widths(columns)
    n = len(cols)
    share, rows = tokens // (2 * ny), tokens // nz
    yh, zh = ny // 4, nz // 4

    vmem = lambda shape, dtype=BF: pltpu.VMEM(shape, dtype)

    def ring(hops, block):
        return [
            (2, max(hops - 1, 1)) + block,
            (2, max(hops - 1, 1)) + block,
            block,
            (2,) + block,
            (2,) + block,
        ]

    z_block = (4 * rows, LANES)
    scratch = [
        vmem((2, 2, tokens, LANES)),
        vmem((2, 2, tokens, LANES)),
        vmem((4, LANES, tokens)),
        vmem((32, columns)),
        vmem((nz,) + z_block, F32),
        vmem((nz,) + z_block),
        vmem((2, 2 * rows, LANES), F32),
        vmem((2, 2 * rows, LANES), F32),
    ]
    z_ring = ring(zh, z_block)
    z_ring[3] = (2, 2, 2 * rows, LANES)
    scratch += [vmem(shape) for shape in z_ring]
    for shape, dtype in (
        (lambda w: (2, 4, LANES, w), BF),
        (lambda w: (2, ny, 2 * share, w), F32),
        (lambda w: (ny, 2 * share, w), F32),
        (lambda w: (ny, 2 * share, w), BF),
        (lambda w: (2, ny, 2 * share, w), BF),
        (lambda w: (4, 2, LANES, w), F32),
        (lambda w: (4, 2, LANES, w), BF),
        (lambda w: (6, LANES, w), BF),
        (lambda w: (2, LANES, w), BF),
    ):
        scratch += [vmem(shape(w), dtype) for w in cols]
    for j in range(5):
        scratch += [vmem(ring(yh, (2 * share, w))[j]) for w in cols]
    dma = pltpu.SemaphoreType.DMA
    scratch += [dma((2 * n + 4,)), dma((2,)), dma((2,)), dma((GROUP - 1,)), dma((GROUP - 1,))]
    scratch += [dma, dma, dma((2,)), dma((2,))]
    for shape in ((n, 4), (n,), (n, 4 * yh - 1), (n, ny - 1), (n,), (n, 6), (6 * zh - 4,)):
        scratch += [dma(shape), dma(shape)]
    scratch += [dma((2, 2)), dma((2, 2))]

    arrays = (inputs, grad_hidden, gate_weight, up_weight)
    in_hbm = pl.BlockSpec(memory_space=pl.ANY)
    in_vmem = pl.BlockSpec(memory_space=pltpu.VMEM)
    grad_inputs, grad_weights = pl.pallas_call(
        functools.partial(kernel, ny, nz, cols),
        out_shape=(
            jax.ShapeDtypeStruct((rows, features), BF),
            jax.ShapeDtypeStruct((2,) + gate_weight.shape, BF),
        ),
        in_specs=[in_hbm] * 4,
        out_specs=(in_vmem,) * 2,
        scratch_shapes=scratch,
        compiler_params=pltpu.CompilerParams(
            collective_id=0, has_side_effects=True, vmem_limit_bytes=36 * 2**20
        ),
        name="step",
    )(*(pltpu.with_memory_space_constraint(a, pltpu.HBM) for a in arrays))
    return grad_inputs, grad_weights[0], grad_weights[1]


def solution(mesh):
    placed = (
        P("dmod", "tok"),
        P("dmod", "hid"),
        P(("tok", "dmod"), "hid"),
        P(("tok", "dmod"), "hid"),
    )
    return jax.shard_map(
        functools.partial(shards, mesh.shape["tok"] // 2, mesh.shape["hid"]),
        mesh=mesh,
        in_specs=placed,
        out_specs=(P(("dmod", "hid"), "tok"), P(("tok", "dmod"), "hid"), P(("tok", "dmod"), "hid")),
        check_vma=False,
    )
```

```python
import functools

import jax
import jax.numpy as jnp
from jax import lax
from jax.experimental import pallas as pl
from jax.experimental.pallas import tpu as pltpu
from jax.sharding import PartitionSpec as P

BF, F32 = jnp.bfloat16, jnp.float32
LANES = 128
GROUP = 4
SIGNS = (1, -1)


def contract(a, b, dims):
    return lax.dot_general(a, b, (dims, ((), ())), preferred_element_type=F32)


def widths(columns):
    tiles = columns // LANES
    return [2 * LANES] * (tiles // 2) + [LANES] * (tiles % 2)


def kernel(ny, nz, cols, x_ref, gh_ref, wg_ref, wu_ref, dx_ref, dw_ref, *scratch):
    n = len(cols)
    starts = [sum(cols[:i]) for i in range(n)]
    it = iter(scratch)
    take = lambda count: [next(it) for _ in range(count)]
    xs, xg, xt, ghw, zf, zs, ze, fx = take(8)
    z_far, z_near, z_anti, z_hub, z_hubs = take(5)
    wb, pb, pr, ys, gb, dwf, dws, dwr, dwh = (take(n) for _ in range(9))
    y_far, y_near, y_anti, y_hub, y_hubs = (take(n) for _ in range(5))
    in_s, x_s, x_r, t_s, t_r, gh_s, gh_r, f_s, f_r = take(9)
    w_s, w_r, p_s, p_r, ys_s, ys_r, g_s, g_r, k_s, k_r, d_s, d_r, zs_s, zs_r, e_s, e_r = take(16)

    tok, dmod, z = lax.axis_index("tok"), lax.axis_index("dmod"), lax.axis_index("hid")
    xl, y, xh, c = lax.div(tok, ny), lax.rem(tok, ny), lax.div(dmod, 2), lax.rem(dmod, 2)
    other = 1 - c
    x = dmod - c + xl
    q = 2 * xl + xh
    tokens = x_ref.shape[0]
    share = tokens // (2 * ny)
    rows = tokens // nz
    home = c == xl

    def at(xl_=xl, xh_=xh, y_=y, c_=c, z_=z):
        return {"tok": xl_ * ny + y_, "dmod": xh_ * 2 + c_, "hid": z_}

    def along_x(k):
        xk = lax.rem(x + 4 + k, 4)
        low, high = lax.rem(xk, 2), lax.div(xk, 2)
        return 2 * low + high, at(xl_=low, xh_=high)

    def along(axis, k):
        if axis == "y":
            return lax.rem(y + ny + k, ny)
        return lax.rem(z + nz + k, nz)

    def there(axis, k):
        return at(y_=along("y", k)) if axis == "y" else at(z_=along("z", k))

    def send(src, dst, send_sem, recv_sem, target):
        copy = pltpu.make_async_remote_copy(
            src_ref=src, dst_ref=dst, send_sem=send_sem, recv_sem=recv_sem,
            device_id=target, device_id_type=pl.DeviceIdType.MESH,
        )
        copy.start()
        return copy

    def arrived(dst, sem):
        pltpu.make_async_copy(dst, dst, sem).wait()

    sent = arrived
    pending = []

    barrier = pltpu.get_barrier_semaphore()
    y_hops, z_hops = ny // 4, nz // 4
    y_off = sorted({s * k % ny for k in range(1, y_hops + 1) for s in SIGNS})
    z_off = sorted({s * k % nz for k in range(1, max(z_hops, GROUP - 1) + 1) for s in SIGNS} - {0})
    peers = [at(c_=other), at(xl_=1 - xl, c_=other)] + [along_x(k)[1] for k in SIGNS]
    peers += [there("y", k) for k in y_off] + [there("z", k) for k in z_off]
    for k in sorted({s * z_hops % nz for s in SIGNS}):
        for a, b in ((xl, other), (1 - xl, c), (1 - xl, other)):
            peers.append(at(xl_=a, c_=b, z_=along("z", k)))
    local = []

    def bring(src, dst):
        copy = pltpu.make_async_copy(src, dst, in_s.at[len(local)])
        copy.start()
        local.append(copy)

    def bring_weights(i):
        span = pl.ds(starts[i], cols[i])
        bring(wg_ref.at[:, span], wb[i].at[0, q])
        bring(wu_ref.at[:, span], wb[i].at[1, q])

    bring_weights(0)
    for h in range(2):
        for cc in range(2):
            bring(x_ref.at[:, pl.ds((2 * h + cc) * LANES, LANES)], xs.at[cc, h])
    first_in = len(local)
    for peer in peers[::-1]:
        pl.semaphore_signal(barrier, 1, device_id=peer, device_id_type=pl.DeviceIdType.MESH)
    for i in range(1, n):
        bring_weights(i)

    def window(core):
        turn = core * ny + y
        first = pl.multiple_of(2 * share * (turn // 2) + 16 * (turn % 2), 16)
        return gh_ref.at[pl.ds(first, 32), :]

    own_gh = pltpu.make_async_copy(window(c), ghw, gh_r)

    @pl.when(home)
    def _():
        own_gh.start()

    for copy in local[:first_in]:
        copy.wait()

    @pl.when(home)
    def _():
        xg[xl] = xs[c]

    pl.semaphore_wait(barrier, len(peers))

    def weights_out(i):
        own = wb[i].at[:, q]
        for slot, k in enumerate(SIGNS):
            pending.append(send(own, own, w_s.at[i, slot], w_r.at[i, slot], along_x(k)[1]))

    part = tokens // GROUP
    turn = lax.rem(z, GROUP)

    def part_of(slab, j):
        return slab.at[:, pl.ds(pl.multiple_of(j * part, part), part)]

    to_core = (xs.at[other], xg.at[xl], x_s.at[0], x_r.at[0], at(c_=other))
    to_gh = (window(other), ghw, gh_s, gh_r, at(c_=other))
    to_chip = [
        (part_of(xs.at[cc], turn), part_of(xg.at[xl], turn), x_s.at[cc], x_r.at[1],
         at(xl_=1 - xl, c_=cc))
        for cc in range(2)
    ]

    @pl.when(home)
    def _():
        send(*to_core)
        send(*to_gh)

    @pl.when(jnp.logical_not(home))
    def _():
        for args in to_chip:
            send(*args)

    weights_out(0)
    for copy in local[first_in:]:
        copy.wait()
    weights_out(1)

    def features():
        mine = part_of(xg.at[1 - xl], turn)
        arrived(mine, x_r.at[1])
        for k in range(1, GROUP):
            mate = z - turn + lax.rem(turn + k, GROUP)
            pending.append(send(mine, mine, t_s.at[k - 1], t_r.at[k - 1], at(z_=mate)))

    def features_done():
        for k in range(1, GROUP):
            arrived(part_of(xg.at[1 - xl], lax.rem(turn + GROUP - k, GROUP)), t_r.at[k - 1])

        @pl.when(jnp.logical_not(home))
        def _():
            arrived(xg.at[xl], x_r.at[0])

        for b in range(4):
            xt[b] = xg[b // 2, b % 2].astype(F32).T.astype(BF)

    def weights_on(i):
        for slot, k in enumerate(SIGNS):
            qk = along_x(-k)[0]
            arrived(wb[i].at[:, qk], w_r.at[i, slot])
            block = wb[i].at[slot, qk]
            pending.append(
                send(block, block, w_s.at[i, 2 + slot], w_r.at[i, 2 + slot], along_x(k)[1])
            )
        if i + 2 < n:
            weights_out(i + 2)

    def partial(i):
        qk = along_x(2)[0]
        for slot in range(2):
            arrived(wb[i].at[slot, qk], w_r.at[i, 2 + slot])
        wide = jnp.concatenate([xg[b // 2, b % 2] for b in range(4)], axis=1)
        for m in range(2):
            w = wb[i][m].reshape(4 * LANES, cols[i])
            block = contract(wide, w, ((1,), (0,))).reshape(2, ny, share, cols[i])
            pb[i][:, :, m * share : (m + 1) * share] = block
        pending.append(send(pb[i].at[other], pr[i], p_s.at[i], p_r.at[i], at(c_=other)))

    def reduce_start(axis, hops, src, far, near, anti, s_sem, r_sem, cuts=1):
        place = lambda k: along(axis, k)
        way = 2 * lax.rem(y if axis == "y" else z, 2) - 1
        lines = src.shape[1] // cuts
        for cut in range(cuts):
            part = pl.ds(cut * lines, lines)
            for j in range(hops - 1, 0, -1):
                for si, s in enumerate(SIGNS):
                    slot = (si * (hops - 1) + j - 1) * cuts + cut
                    pending.append(
                        send(src.at[place(s * (j + hops)), part], far.at[si, j - 1, part],
                             s_sem.at[slot], r_sem.at[slot], there(axis, s * j))
                    )
            slot = 2 * (hops - 1) * cuts + cut
            pending.append(
                send(src.at[place(2 * hops), part], anti.at[part], s_sem.at[slot], r_sem.at[slot],
                     there(axis, way * hops))
            )
        for j in range(1, hops):
            for si, s in enumerate(SIGNS):
                slot = (2 * hops - 1) * cuts + si * (hops - 1) + j - 1
                pending.append(
                    send(src.at[place(s * j)], near.at[si, j - 1], s_sem.at[slot], r_sem.at[slot],
                         there(axis, s * j))
                )

    def reduce_relay(axis, hops, own, far, anti, hubs, r_sem, deliver, cut=0, cuts=1):
        odd = lax.rem(y if axis == "y" else z, 2)
        lines = hubs.shape[1] // cuts
        part = pl.ds(cut * lines, lines)
        for j in range(1, hops):
            for si in range(2):
                slot = (si * (hops - 1) + j - 1) * cuts + cut
                arrived(far.at[si, j - 1, part], r_sem.at[slot])
        arrived(anti.at[part], r_sem.at[2 * (hops - 1) * cuts + cut])
        for first in (True, False):
            si = 1 - odd if first else odd
            way = 1 - 2 * si
            total = own(along(axis, way * hops), part)
            for j in range(1, hops):
                total = total + far[si, j - 1, part].astype(F32)
            if first:
                total = total + anti[part].astype(F32)
            hubs[si, part] = total.astype(BF)
            deliver(si, along(axis, way * hops))

    def reduce_near(axis, hops, own, near, r_sem, cuts=1):
        total = own(y if axis == "y" else z, slice(None))
        for j in range(1, hops):
            for si in range(2):
                slot = (2 * hops - 1) * cuts + si * (hops - 1) + j - 1
                arrived(near.at[si, j - 1], r_sem.at[slot])
                total = total + near[si, j - 1].astype(F32)
        return total

    def own_sum(i):
        return lambda yk, part: pb[i][c, yk, part] + pr[i][yk, part]

    def scatter(i):
        arrived(pr[i], p_r.at[i])
        ys[i][...] = (pb[i][c] + pr[i][...]).astype(BF)
        reduce_start("y", y_hops, ys[i], y_far[i], y_near[i], y_anti[i], ys_s.at[i], ys_r.at[i])

    y_slot = 4 * (y_hops - 1) + 1

    def relay(i):
        def deliver(si, yk):
            src, slot = y_hubs[i].at[si], y_slot + si
            pending.append(
                send(src, y_hub[i].at[si], ys_s.at[i, slot], ys_r.at[i, slot], at(y_=yk))
            )

        reduce_relay("y", y_hops, own_sum(i), y_far[i], y_anti[i], y_hubs[i], ys_r.at[i], deliver)

    def activate(i):
        if i == 0:
            @pl.when(home)
            def _():
                own_gh.wait()

            @pl.when(jnp.logical_not(home))
            def _():
                arrived(ghw, gh_r)

        total = reduce_near("y", y_hops, own_sum(i), y_near[i], ys_r.at[i])
        for si in range(2):
            arrived(y_hub[i].at[si], ys_r.at[i, y_slot + si])
            total = total + y_hub[i][si].astype(F32)
        gate, up = total[:share], total[share:]
        upstream = ghw[:, starts[i] : starts[i] + cols[i]].astype(F32)
        upstream = jnp.where((c * ny + y) % 2 == 1, upstream[8 : 8 + share], upstream[:share])
        sigma = jax.nn.sigmoid(gate)
        grad_gate = upstream * up * sigma * (1.0 + gate * (1.0 - sigma))
        grad_up = upstream * gate * sigma
        gb[i][c, y] = jnp.concatenate([grad_gate, grad_up], axis=0).astype(BF)
        own = gb[i].at[c, y]
        for k in range(y_hops, 0, -1):
            for s in SIGNS:
                slot = s * k % ny - 1
                pending.append(send(own, own, g_s.at[i, slot], g_r.at[i, slot], there("y", s * k)))

    def spread(i):
        for s in SIGNS:
            block = gb[i].at[c, along("y", -s * y_hops)]
            arrived(block, g_r.at[i, s * y_hops % ny - 1])
            for j in range(1, y_hops):
                slot = s * (j + y_hops) % ny - 1
                pending.append(send(block, block, g_s.at[i, slot], g_r.at[i, slot], there("y", s * j)))
        way = 2 * lax.rem(y, 2) - 1
        block = gb[i].at[c, along("y", -way * y_hops)]
        slot = 2 * y_hops - 1
        pending.append(
            send(block, block, g_s.at[i, slot], g_r.at[i, slot], there("y", way * y_hops))
        )

    def gather(i):
        for k in range(1, ny):
            if k not in (y_hops, ny - y_hops):
                arrived(gb[i].at[c, along("y", -k)], g_r.at[i, k - 1])
        pending.append(send(gb[i].at[c], gb[i].at[c], k_s.at[i], k_r.at[i], at(c_=other)))

    def grads_of(i):
        both = gb[i][...].astype(F32).reshape(2 * ny, 2 * share, cols[i])
        grad_gate = both[:, :share].reshape(tokens, cols[i]).astype(BF)
        grad_up = both[:, share:].reshape(tokens, cols[i]).astype(BF)
        return grad_gate, grad_up

    def input_part(i):
        arrived(gb[i].at[other], k_r.at[i])
        grads = grads_of(i)
        for b in range(4):
            total = 0.0
            for m, grad in enumerate(grads):
                total = total + contract(grad, wb[i][m, b], ((1,), (1,)))
            total = total.reshape(nz, rows, LANES)
            span = slice(b * rows, (b + 1) * rows)
            zf[:, span] = total if i == 0 else zf[:, span] + total

    def weight_part(i):
        for m, grad in enumerate(grads_of(i)):
            for b in range(4):
                dwf[i][b, m] = contract(xt[b], grad, ((1,), (0,)))
        dws[i][...] = dwf[i][...].astype(BF)
        q2 = along_x(2)[0]
        for m, k in enumerate(SIGNS):
            pending.append(
                send(dws[i].at[q2, m], dwr[i].at[m], d_s.at[i, m], d_r.at[i, m], along_x(k)[1])
            )
        for m, k in enumerate(SIGNS):
            qk, target = along_x(k)
            pending.append(
                send(dws[i].at[qk, 1 - m], dwr[i].at[2 + m], d_s.at[i, 2 + m], d_r.at[i, 2 + m], target)
            )

    def weight_relay(i):
        for m, k in enumerate(SIGNS):
            qk, target = along_x(k)
            arrived(dwr[i].at[m], d_r.at[i, m])
            dwh[i][m] = (dwf[i][qk, m] + dwr[i][m].astype(F32)).astype(BF)
            pending.append(
                send(dwh[i].at[m], dwr[i].at[4 + m], d_s.at[i, 4 + m], d_r.at[i, 4 + m], target)
            )

    def weight_out(i):
        span = slice(starts[i], starts[i] + cols[i])
        for m in range(2):
            total = dwf[i][q, m]
            for slot in (3 - m, 4 + m):
                arrived(dwr[i].at[slot], d_r.at[i, slot])
                total = total + dwr[i][slot].astype(F32)
            dw_ref[m, :, span] = total.astype(BF)

    own_input = lambda zk, part: zf[zk, part]

    def input_start():
        zs[...] = zf[...].astype(BF)
        reduce_start("z", z_hops, zs, z_far, z_near, z_anti, zs_s, zs_r, 2)

    half = 2 * rows

    def input_relay(to):
        def deliver(si, zk):
            target = at(xl_=to, c_=xl, z_=zk)
            src = z_hubs.at[si, pl.ds(to * half, half)]
            pending.append(send(src, z_hub.at[si, c], e_s.at[si, to], e_r.at[si, c], target))

        reduce_relay("z", z_hops, own_input, z_far, z_anti, z_hubs, zs_r, deliver, to, 2)

    def input_near():
        total = reduce_near("z", z_hops, own_input, z_near, zs_r, 2)
        ze[...] = total.reshape(2, half, LANES)
        target = at(xl_=1 - xl, c_=xl)
        pending.append(send(ze.at[1 - xl], fx.at[c], f_s.at[0], f_r.at[c], target))

        @pl.when(home)
        def _():
            fx[c] = ze[xl]

        @pl.when(jnp.logical_not(home))
        def _():
            send(ze.at[xl], fx.at[c], f_s.at[1], f_r.at[c], at(c_=other))

    ready = {
        weights_on: (9, 11.8, 18.2, 20.3),
        partial: (14.7, 18.7, 22.5, 23.1),
        scatter: (16.2, 22.2, 24.6, 26.1),
        relay: (21.5, 26.4, 27.3, 30.3),
        activate: (25.2, 31.7, 32.9, 35),
        spread: (29.2, 36.6, 37.4, 38.1),
        gather: (34, 39.3, 41.2, 43),
        input_part: (35.6, 42, 43.2, 44.3),
        weight_part: (36.8, 42.4, 43.6, 45.1),
        weight_relay: (40.7, 45.7, 46.8, 49.6),
        weight_out: (45.5, 55, 56, 57),
    }
    late = {features: 5, features_done: 14.6, input_start: 44.5, input_near: 53}
    order = [(when, stage, None) for stage, when in late.items()]
    order += [(48.5, input_relay, 0), (51.6, input_relay, 1)]
    for stage, times in ready.items():
        shift = len(times) - n
        order += [(times[i if i < n - 1 else i + shift], stage, i) for i in range(n)]
    for _, stage, i in sorted(order, key=lambda entry: entry[0]):
        stage() if i is None else stage(i)

    recent = 24
    for copy in pending[:-recent]:
        copy.wait_send()

    @pl.when(home)
    def _():
        sent(xs.at[other], x_s.at[0])
        sent(window(other), gh_s)

    @pl.when(jnp.logical_not(home))
    def _():
        for cc in range(2):
            sent(part_of(xs.at[cc], turn), x_s.at[cc])

    @pl.when(jnp.logical_not(home))
    def _():
        arrived(fx.at[c], f_r.at[c])

    arrived(fx.at[other], f_r.at[other])
    for si in range(2):
        for cc in range(2):
            arrived(z_hub.at[si, cc], e_r.at[si, cc])
    for cc in range(2):
        got = fx[cc] + z_hub[0, cc].astype(F32) + z_hub[1, cc].astype(F32)
        for h in range(2):
            at_col = (2 * h + cc) * LANES
            dx_ref[:, at_col : at_col + LANES] = got[h * rows : (h + 1) * rows].astype(BF)

    @pl.when(jnp.logical_not(home))
    def _():
        sent(ze.at[xl], f_s.at[1])

    for copy in pending[-recent:]:
        copy.wait_send()


def shards(ny, nz, inputs, grad_hidden, gate_weight, up_weight):
    tokens, features = inputs.shape
    columns = gate_weight.shape[1]
    cols = widths(columns)
    n = len(cols)
    share, rows = tokens // (2 * ny), tokens // nz
    yh, zh = ny // 4, nz // 4

    vmem = lambda shape, dtype=BF: pltpu.VMEM(shape, dtype)

    def ring(hops, block):
        return [
            (2, max(hops - 1, 1)) + block,
            (2, max(hops - 1, 1)) + block,
            block,
            (2,) + block,
            (2,) + block,
        ]

    z_block = (4 * rows, LANES)
    scratch = [
        vmem((2, 2, tokens, LANES)),
        vmem((2, 2, tokens, LANES)),
        vmem((4, LANES, tokens)),
        vmem((32, columns)),
        vmem((nz,) + z_block, F32),
        vmem((nz,) + z_block),
        vmem((2, 2 * rows, LANES), F32),
        vmem((2, 2 * rows, LANES), F32),
    ]
    z_ring = ring(zh, z_block)
    z_ring[3] = (2, 2, 2 * rows, LANES)
    scratch += [vmem(shape) for shape in z_ring]
    for shape, dtype in (
        (lambda w: (2, 4, LANES, w), BF),
        (lambda w: (2, ny, 2 * share, w), F32),
        (lambda w: (ny, 2 * share, w), F32),
        (lambda w: (ny, 2 * share, w), BF),
        (lambda w: (2, ny, 2 * share, w), BF),
        (lambda w: (4, 2, LANES, w), F32),
        (lambda w: (4, 2, LANES, w), BF),
        (lambda w: (6, LANES, w), BF),
        (lambda w: (2, LANES, w), BF),
    ):
        scratch += [vmem(shape(w), dtype) for w in cols]
    for j in range(5):
        scratch += [vmem(ring(yh, (2 * share, w))[j]) for w in cols]
    dma = pltpu.SemaphoreType.DMA
    scratch += [dma((2 * n + 4,)), dma((2,)), dma((2,)), dma((GROUP - 1,)), dma((GROUP - 1,))]
    scratch += [dma, dma, dma((2,)), dma((2,))]
    for shape in ((n, 4), (n,), (n, 4 * yh - 1), (n, ny - 1), (n,), (n, 6), (6 * zh - 4,)):
        scratch += [dma(shape), dma(shape)]
    scratch += [dma((2, 2)), dma((2, 2))]

    arrays = (inputs, grad_hidden, gate_weight, up_weight)
    in_hbm = pl.BlockSpec(memory_space=pl.ANY)
    in_vmem = pl.BlockSpec(memory_space=pltpu.VMEM)
    grad_inputs, grad_weights = pl.pallas_call(
        functools.partial(kernel, ny, nz, cols),
        out_shape=(
            jax.ShapeDtypeStruct((rows, features), BF),
            jax.ShapeDtypeStruct((2,) + gate_weight.shape, BF),
        ),
        in_specs=[in_hbm] * 4,
        out_specs=(in_vmem,) * 2,
        scratch_shapes=scratch,
        compiler_params=pltpu.CompilerParams(
            collective_id=0, has_side_effects=True, vmem_limit_bytes=36 * 2**20
        ),
        name="step",
    )(*(pltpu.with_memory_space_constraint(a, pltpu.HBM) for a in arrays))
    return grad_inputs, grad_weights[0], grad_weights[1]


def solution(mesh):
    placed = (
        P("dmod", "tok"),
        P("dmod", "hid"),
        P(("tok", "dmod"), "hid"),
        P(("tok", "dmod"), "hid"),
    )
    return jax.shard_map(
        functools.partial(shards, mesh.shape["tok"] // 2, mesh.shape["hid"]),
        mesh=mesh,
        in_specs=placed,
        out_specs=(P(("dmod", "hid"), "tok"), P(("tok", "dmod"), "hid"), P(("tok", "dmod"), "hid")),
        check_vma=False,
    )
```
